32 devices in a mesh: mirror: 2 (over y), slab: 8 (over z, x), cols: 2 (over core).
Axes of the slice: x: 2, y: 2, z: 4, core: 2. Of those that a mesh axis runs over, the one named last changes fastest.
Arguments:
- right_side: float32 [2, 1024, 8192], P('mirror', 'slab', 'cols'), parts along dimension 2, may hold values from -6 to 6
- analysis: float32 [2, 1024, 1024], P('mirror'), may hold values from -0.1875 to 0.1875
- synthesis: float32 [2, 1024, 1024], P('mirror'), may hold values from -0.1875 to 0.1875
- negated_eigen: float32 [2, 1024], P('mirror'), may hold values from 0.25 to 4
- wave_square: float32 [8192], P(('cols', 'slab')), parts along dimension 0, may hold values from 0.25 to 4
Outputs:
- solution: float32 [2, 1024, 8192], P('mirror', 'slab', 'cols'), parts along dimension 2
The draws below stay inside these ranges and needn't reach their ends.
There are 2 independent parts, one for each index of `cols`. The reference program is written for one: setup_inputs(seed, part) draws one part's arguments, and reference() takes and returns one part's arrays. A program takes and returns all parts, laid end to end along the dimension named above; an argument that names none is the same for every part. Nothing has to cross between parts.
All inputs are finite; a program needn't handle non-finite values.
Results may differ from the reference program's by a relative error of at most 0.0001.
Values sent between devices are 32-bit elements; how exact they have to be, the bound alone decides.
A program may use at most 64 MiB of HBM per device.

```python
import math
import jax
import jax.numpy as jnp
from jax import lax

HALF = 1024
MODES = 4096


def levels(key, dims, shards, least, high):
    gain = 1.0
    for axis_at, parts in shards:
        heights = jax.random.uniform(jax.random.fold_in(jax.random.fold_in(key, 6), axis_at), (parts,), jnp.float32, least / len(shards), high / len(shards))
        gain = gain * jnp.repeat(jnp.exp(heights), dims[axis_at] // parts).reshape((-1,) + (1,) * (len(dims) - 1 - axis_at))
    return gain


def bell_draw(rng, dims, width, most, shards=(), held_as=jnp.bfloat16):
    result = width * jax.random.normal(rng, dims, jnp.float32)
    if shards:
        result = result * levels(rng, dims, shards, -0.22, 0.18)
    return jnp.clip(result, -most, most).astype(held_as)


def setup_inputs(seed: int = 0, part: int = 0) -> dict:
    key_list = jax.random.split(jax.random.key(seed), 6)
    part_keys = jax.random.split(jax.random.fold_in(key_list[5], part), 6)
    return {
        "right_side": bell_draw(part_keys[0], (2, HALF, MODES), 1.0, 6.0, ((0, 2), (1, 8)), jnp.float32),
        "analysis": bell_draw(key_list[1], (2, HALF, HALF), HALF ** -0.5, 0.1875, ((0, 2),), jnp.float32),
        "synthesis": bell_draw(key_list[2], (2, HALF, HALF), HALF ** -0.5, 0.1875, ((0, 2),), jnp.float32),
        "negated_eigen": jnp.clip(jnp.exp(math.log(4.0) - 2.7725887 * jax.random.uniform(key_list[3], (2, HALF), jnp.float32) ** levels(key_list[3], (2, HALF), ((0, 2),), -0.2, 0.2)), 0.25, 4.0),
        "wave_square": jnp.clip(jnp.exp(math.log(4.0) - 2.7725887 * jax.random.uniform(part_keys[4], (MODES,), jnp.float32) ** levels(part_keys[4], (MODES,), ((0, 8),), -0.2, 0.2)), 0.25, 4.0),
    }


def reference(right_side, analysis, synthesis, negated_eigen, wave_square):
    parity_fields = []
    for parity in range(2):
        folded = (right_side[0] + (1 - 2 * parity) * right_side[1]) * 0.5
        coefficients = jnp.dot(analysis[parity], folded, precision=lax.Precision.HIGHEST, preferred_element_type=jnp.float32)
        scaled = coefficients / (negated_eigen[parity][:, None] + wave_square[None, :])
        parity_fields.append(-jnp.dot(synthesis[parity], scaled, precision=lax.Precision.HIGHEST, preferred_element_type=jnp.float32))
    return jnp.stack((parity_fields[0] + parity_fields[1], parity_fields[0] - parity_fields[1]))
```

```python
import functools

import jax
import jax.numpy as jnp
from jax import lax
from jax.experimental import pallas as pl
from jax.experimental.pallas import tpu as pltpu
from jax.sharding import PartitionSpec as P

MESH = pl.DeviceIdType.MESH
PAIRS = 2
TILE = 256
SWAP_A, SPREAD_A, SPREAD_B, SWAP_B, BACK_SWAP_B, BACK_SPREAD_B, BACK_SPREAD_A, BACK_SWAP_A = range(8)
GROUPS = 8


def split(value):
    high = value.astype(jnp.bfloat16)
    return high, (value - high.astype(jnp.float32)).astype(jnp.bfloat16)


def kernel(
    n,
    field,
    analysis,
    synthesis,
    eigen,
    wave,
    out,
    own,
    staged,
    matrices,
    swapped_a,
    folded_a,
    landed_a,
    landed_b,
    swapped_b,
    right,
    scaled,
    solved_a,
    solved_b,
    back_a,
    back_swapped_a,
    back_swapped_b,
    combined_b,
    combined_a,
    send_sem,
    recv_sem,
    load_sem,
    own_b_sem,
    store_sem,
):
    rows = field.shape[1]
    width = field.shape[2] // n
    w = width // (2 * PAIRS)
    height = analysis.shape[1]
    me = lax.axis_index("slab")
    parity = lax.axis_index("mirror")
    sign = (1 - 2 * parity).astype(jnp.float32)
    partner = {"mirror": 1 - parity}

    def offset(i):
        half = (i + 1) // 2
        odd = i % 2
        return n // 2 + odd * half + (1 - odd) * (n - half)

    def target(i):
        return lax.rem(me + offset(i), n)

    def source(i):
        return lax.rem(me + 2 * n - offset(i), n)

    def columns(d, k, b):
        return pl.ds(pl.multiple_of(d * width + (2 * k + b) * w, w), w)

    def remote(src, dst, k, group, sent, received, device):
        return pltpu.make_async_remote_copy(
            src_ref=src,
            dst_ref=dst,
            send_sem=send_sem.at[k * GROUPS + group, sent],
            recv_sem=recv_sem.at[k * GROUPS + group, received],
            device_id=device,
            device_id_type=MESH,
        )

    def swap(src, dst, k, group, d):
        remote(src, dst, k, group, d, d, partner).start()

    def spread(src, dst, k, group, d):
        remote(src, dst, k, group, d, me, {"slab": d}).start()

    def arrived(dst, k, group, s):
        remote(dst, dst, k, group, s, s, partner).wait_recv()

    def each(body):
        def step(i, carry):
            body(i)
            return carry

        lax.fori_loop(0, n - 1, step, 0)

    loads = [
        pltpu.make_async_copy(field.at[0], own, load_sem.at[0]),
        pltpu.make_async_copy(analysis.at[0], staged.at[0], load_sem.at[1]),
        pltpu.make_async_copy(synthesis.at[0], staged.at[1], load_sem.at[2]),
    ]
    own_b = [
        pltpu.make_async_copy(field.at[0, :, columns(me, k, 1)], landed_b.at[k, me], own_b_sem.at[k])
        for k in range(PAIRS)
    ]
    for copy in loads + own_b:
        copy.start()

    barrier = pltpu.get_barrier_semaphore()

    def greet(i):
        pl.semaphore_signal(barrier, inc=1, device_id={"slab": target(i)}, device_id_type=MESH)

    each(greet)
    pl.semaphore_signal(barrier, inc=1, device_id=partner, device_id_type=MESH)
    pl.semaphore_wait(barrier, n)

    def forward_start(k):
        def body(i):
            d = target(i)
            swap(field.at[0, :, columns(d, k, 0)], swapped_a.at[k, d], k, SWAP_A, d)
            spread(field.at[0, :, columns(d, k, 1)], landed_b.at[k, me], k, SPREAD_B, d)

        each(body)
        swap(field.at[0, :, columns(me, k, 0)], swapped_a.at[k, me], k, SWAP_A, me)
        swap(field.at[0, :, columns(me, k, 1)], swapped_b.at[k, me], k, SWAP_B, me)

    def fold_a(k, d):
        arrived(swapped_a.at[k, d], k, SWAP_A, d)
        return (swapped_a[k, d] + sign * own[:, columns(d, k, 0)]) * 0.5

    def forward_relay(k):
        def body(i):
            d = target(i)
            folded_a[k, d] = fold_a(k, d)
            spread(folded_a.at[k, d], landed_a.at[k, me], k, SPREAD_A, d)
            s = source(i)
            arrived(landed_b.at[k, s], k, SPREAD_B, s)
            swap(landed_b.at[k, s], swapped_b.at[k, s], k, SWAP_B, s)

        each(body)
        landed_a[k, me] = fold_a(k, me)
        own_b[k].wait()

    def gather(k):
        def put(s):
            block = pl.ds(pl.multiple_of(s * rows, rows), rows)
            right[0, block, :w], right[1, block, :w] = split(landed_a[k, s])
            arrived(swapped_b.at[k, s], k, SWAP_B, s)
            folded = (swapped_b[k, s] + sign * landed_b[k, s]) * 0.5
            right[0, block, w:], right[1, block, w:] = split(folded)

        put(me)

        def body(i):
            s = source(i)
            arrived(landed_a.at[k, s], k, SPREAD_A, s)
            put(s)

        each(body)

    def product(which, operand, finish):
        def step(t, carry):
            block = pl.ds(pl.multiple_of(t * TILE, TILE), TILE)
            high, low = matrices[which, 0, block, :], matrices[which, 1, block, :]
            dot = functools.partial(jnp.dot, preferred_element_type=jnp.float32)
            finish(t, block, dot(high, operand[0]) + (dot(high, operand[1]) + dot(low, operand[0])))
            return carry

        lax.fori_loop(0, height // TILE, step, 0)

    def compute(k):
        def scale(t, block, total):
            shift = jnp.broadcast_to(eigen[0:1, block], (2 * w, TILE)).T
            value = total / (shift + wave[0:1, 2 * w * k : 2 * w * (k + 1)])
            scaled[0, block, :], scaled[1, block, :] = split(value)

        def keep(t, block, total):
            per = TILE // rows
            blocks = pl.ds(t * per, per)
            solved_a[k, blocks] = -total[:, :w].reshape(per, rows, w)
            solved_b[k, blocks] = -total[:, w:].reshape(per, rows, w)

        product(0, right, scale)
        product(1, scaled, keep)

    def back_start(k):
        def body(i):
            d = target(i)
            spread(solved_a.at[k, d], back_a.at[k, me], k, BACK_SPREAD_A, d)
            swap(solved_b.at[k, d], back_swapped_b.at[k, d], k, BACK_SWAP_B, d)

        each(body)
        swap(solved_a.at[k, me], back_swapped_a.at[k, me], k, BACK_SWAP_A, me)
        swap(solved_b.at[k, me], back_swapped_b.at[k, me], k, BACK_SWAP_B, me)

    def combine_b(k, d):
        arrived(back_swapped_b.at[k, d], k, BACK_SWAP_B, d)
        combined_b[k, d] = back_swapped_b[k, d] + sign * solved_b[k, d]

    def own_back_b(k):
        return pltpu.make_async_copy(
            combined_b.at[k, me], out.at[0, :, columns(me, k, 1)], store_sem.at[k, n]
        )

    def back_relay(k):
        def body(i):
            d = target(i)
            combine_b(k, d)
            spread(combined_b.at[k, d], out.at[0, :, columns(me, k, 1)], k, BACK_SPREAD_B, d)
            s = source(i)
            arrived(back_a.at[k, s], k, BACK_SPREAD_A, s)
            swap(back_a.at[k, s], back_swapped_a.at[k, s], k, BACK_SWAP_A, s)

        each(body)
        combine_b(k, me)
        own_back_b(k).start()

    def store_a(k, s):
        return pltpu.make_async_copy(
            combined_a.at[k, s], out.at[0, :, columns(s, k, 0)], store_sem.at[k, s]
        )

    def finish(k):
        def put(s, mine):
            arrived(back_swapped_a.at[k, s], k, BACK_SWAP_A, s)
            combined_a[k, s] = back_swapped_a[k, s] + sign * mine[k, s]
            store_a(k, s).start()

        put(me, solved_a)
        each(lambda i: put(source(i), back_a))

    def drain(k):
        def body(i):
            s = source(i)
            arrived(out.at[0, :, columns(s, k, 1)], k, BACK_SPREAD_B, s)
            d = target(i)
            for group in range(GROUPS):
                remote(landed_a.at[k, d], landed_a.at[k, d], k, group, d, d, partner).wait_send()
            store_a(k, s).wait()

        each(body)
        for group in (SWAP_A, SWAP_B, BACK_SWAP_A, BACK_SWAP_B):
            remote(landed_a.at[k, me], landed_a.at[k, me], k, group, me, me, partner).wait_send()
        store_a(k, me).wait()
        own_back_b(k).wait()

    forward_start(0)

    for copy in loads:
        copy.wait()

    def halve(t, carry):
        block = pl.ds(pl.multiple_of(t * TILE, TILE), TILE)
        for which in range(2):
            matrices[which, 0, block, :], matrices[which, 1, block, :] = split(staged[which, block, :])
        return carry

    lax.fori_loop(0, height // TILE, halve, 0)

    for k in range(PAIRS):
        forward_relay(k)
        if k + 1 < PAIRS:
            forward_start(k + 1)
        if k > 0:
            back_start(k - 1)
        gather(k)
        compute(k)
        if k > 0:
            back_relay(k - 1)
    back_start(PAIRS - 1)
    for k in range(PAIRS - 1):
        finish(k)
    back_relay(PAIRS - 1)
    finish(PAIRS - 1)
    for k in range(PAIRS):
        drain(k)


def shards(n, right_side, analysis, synthesis, negated_eigen, wave_square):
    rows, modes = right_side.shape[1:]
    height = analysis.shape[1]
    width = modes // n
    w = width // (2 * PAIRS)
    pieces = pltpu.VMEM((PAIRS, n, rows, w), jnp.float32)
    anywhere = pl.BlockSpec(memory_space=pl.ANY)
    vmem = pl.BlockSpec(memory_space=pltpu.VMEM)
    return pl.pallas_call(
        functools.partial(kernel, n),
        out_shape=jax.ShapeDtypeStruct(right_side.shape, jnp.float32),
        in_specs=[anywhere, anywhere, anywhere, vmem, vmem],
        out_specs=anywhere,
        scratch_shapes=[
            pltpu.VMEM((rows, modes), jnp.float32),
            pltpu.VMEM((2, height, height), jnp.float32),
            pltpu.VMEM((2, 2, height, height), jnp.bfloat16),
        ]
        + [pieces] * 5
        + [pltpu.VMEM((2, height, 2 * w), jnp.bfloat16)] * 2
        + [pieces] * 7
        + [
            pltpu.SemaphoreType.DMA((PAIRS * GROUPS, n)),
            pltpu.SemaphoreType.DMA((PAIRS * GROUPS, n)),
            pltpu.SemaphoreType.DMA((3,)),
            pltpu.SemaphoreType.DMA((PAIRS,)),
            pltpu.SemaphoreType.DMA((PAIRS, n + 1)),
        ],
        compiler_params=pltpu.CompilerParams(
            collective_id=0, has_side_effects=True, vmem_limit_bytes=56 * 2**20
        ),
    )(right_side, analysis, synthesis, negated_eigen, wave_square[None])


def solution(mesh):
    return jax.shard_map(
        functools.partial(shards, mesh.shape["slab"]),
        mesh=mesh,
        in_specs=(
            P("mirror", "slab", "cols"),
            P("mirror", None, None),
            P("mirror", None, None),
            P("mirror", None),
            P(("cols", "slab")),
        ),
        out_specs=P("mirror", "slab", "cols"),
        check_vma=False,
    )
```

```python
import functools

import jax
import jax.numpy as jnp
from jax import lax
from jax.experimental import pallas as pl
from jax.experimental.pallas import tpu as pltpu
from jax.sharding import PartitionSpec as P

MESH = pl.DeviceIdType.MESH
PAIRS = 2
TILE = 256
SWAP_A, SPREAD_A, SPREAD_B, SWAP_B, BACK_SWAP_B, BACK_SPREAD_B, BACK_SPREAD_A, BACK_SWAP_A = range(8)
GROUPS = 8


def split(value):
    high = value.astype(jnp.bfloat16)
    return high, (value - high.astype(jnp.float32)).astype(jnp.bfloat16)


def kernel(
    n,
    field,
    analysis,
    synthesis,
    eigen,
    wave,
    out,
    own,
    staged,
    matrices,
    swapped_a,
    folded_a,
    landed_a,
    landed_b,
    swapped_b,
    right,
    scaled,
    solved_a,
    solved_b,
    back_a,
    back_swapped_a,
    back_swapped_b,
    combined_b,
    combined_a,
    send_sem,
    recv_sem,
    load_sem,
    own_b_sem,
    store_sem,
):
    rows = field.shape[1]
    width = field.shape[2] // n
    w = width // (2 * PAIRS)
    height = analysis.shape[1]
    me = lax.axis_index("slab")
    parity = lax.axis_index("mirror")
    sign = (1 - 2 * parity).astype(jnp.float32)
    partner = {"mirror": 1 - parity}

    def offset(i):
        half = (i + 1) // 2
        odd = i % 2
        return n // 2 + odd * half + (1 - odd) * (n - half)

    def target(i):
        return lax.rem(me + offset(i), n)

    def source(i):
        return lax.rem(me + 2 * n - offset(i), n)

    def columns(d, k, b):
        return pl.ds(pl.multiple_of(d * width + (2 * k + b) * w, w), w)

    def remote(src, dst, k, group, sent, received, device):
        return pltpu.make_async_remote_copy(
            src_ref=src,
            dst_ref=dst,
            send_sem=send_sem.at[k * GROUPS + group, sent],
            recv_sem=recv_sem.at[k * GROUPS + group, received],
            device_id=device,
            device_id_type=MESH,
        )

    def swap(src, dst, k, group, d):
        remote(src, dst, k, group, d, d, partner).start()

    def spread(src, dst, k, group, d):
        remote(src, dst, k, group, d, me, {"slab": d}).start()

    def arrived(dst, k, group, s):
        remote(dst, dst, k, group, s, s, partner).wait_recv()

    def each(body, start=0, stop=n - 1):
        def step(i, carry):
            body(i)
            return carry

        lax.fori_loop(start, stop, step, 0)

    def whole(relay):
        body, last = relay
        each(body)
        last()

    loads = [
        pltpu.make_async_copy(field.at[0], own, load_sem.at[0]),
        pltpu.make_async_copy(analysis.at[0], staged.at[0], load_sem.at[1]),
        pltpu.make_async_copy(synthesis.at[0], staged.at[1], load_sem.at[2]),
    ]
    own_b = [
        pltpu.make_async_copy(field.at[0, :, columns(me, k, 1)], landed_b.at[k, me], own_b_sem.at[k])
        for k in range(PAIRS)
    ]
    for copy in loads + own_b:
        copy.start()

    barrier = pltpu.get_barrier_semaphore()

    def greet(i):
        pl.semaphore_signal(barrier, inc=1, device_id={"slab": target(i)}, device_id_type=MESH)

    each(greet)
    pl.semaphore_signal(barrier, inc=1, device_id=partner, device_id_type=MESH)
    pl.semaphore_wait(barrier, n)

    def forward_start(k):
        def body(i):
            d = target(i)
            swap(field.at[0, :, columns(d, k, 0)], swapped_a.at[k, d], k, SWAP_A, d)
            spread(field.at[0, :, columns(d, k, 1)], landed_b.at[k, me], k, SPREAD_B, d)

        each(body)
        swap(field.at[0, :, columns(me, k, 0)], swapped_a.at[k, me], k, SWAP_A, me)
        swap(field.at[0, :, columns(me, k, 1)], swapped_b.at[k, me], k, SWAP_B, me)

    def fold_a(k, d):
        arrived(swapped_a.at[k, d], k, SWAP_A, d)
        return (swapped_a[k, d] + sign * own[:, columns(d, k, 0)]) * 0.5

    def forward_relay(k):
        def body(i):
            d = target(i)
            folded_a[k, d] = fold_a(k, d)
            spread(folded_a.at[k, d], landed_a.at[k, me], k, SPREAD_A, d)
            s = source(i)
            arrived(landed_b.at[k, s], k, SPREAD_B, s)
            swap(landed_b.at[k, s], swapped_b.at[k, s], k, SWAP_B, s)

        def last():
            landed_a[k, me] = fold_a(k, me)
            own_b[k].wait()

        return body, last

    def gather(k):
        def put(s):
            block = pl.ds(pl.multiple_of(s * rows, rows), rows)
            right[0, block, :w], right[1, block, :w] = split(landed_a[k, s])
            arrived(swapped_b.at[k, s], k, SWAP_B, s)
            folded = (swapped_b[k, s] + sign * landed_b[k, s]) * 0.5
            right[0, block, w:], right[1, block, w:] = split(folded)

        put(me)

        def body(i):
            s = source(i)
            arrived(landed_a.at[k, s], k, SPREAD_A, s)
            put(s)

        each(body)

    tiles = height // TILE

    def product(which, operand, finish, beside):
        def step(t, carry):
            block = pl.ds(pl.multiple_of(t * TILE, TILE), TILE)
            high, low = matrices[which, 0, block, :], matrices[which, 1, block, :]
            dot = functools.partial(jnp.dot, preferred_element_type=jnp.float32)
            finish(t, block, dot(high, operand[0]) + (dot(high, operand[1]) + dot(low, operand[0])))
            at = which * tiles + t
            each(beside, at * (n - 1) // (2 * tiles), (at + 1) * (n - 1) // (2 * tiles))
            return carry

        lax.fori_loop(0, tiles, step, 0)

    def compute(k, relay):
        beside, last = relay

        def scale(t, block, total):
            shift = jnp.broadcast_to(eigen[0:1, block], (2 * w, TILE)).T
            value = total / (shift + wave[0:1, 2 * w * k : 2 * w * (k + 1)])
            scaled[0, block, :], scaled[1, block, :] = split(value)

        def keep(t, block, total):
            per = TILE // rows
            blocks = pl.ds(t * per, per)
            solved_a[k, blocks] = -total[:, :w].reshape(per, rows, w)
            solved_b[k, blocks] = -total[:, w:].reshape(per, rows, w)

        product(0, right, scale, beside)
        product(1, scaled, keep, beside)
        last()

    def back_start(k):
        def body(i):
            d = target(i)
            spread(solved_a.at[k, d], back_a.at[k, me], k, BACK_SPREAD_A, d)
            swap(solved_b.at[k, d], back_swapped_b.at[k, d], k, BACK_SWAP_B, d)

        each(body)
        swap(solved_a.at[k, me], back_swapped_a.at[k, me], k, BACK_SWAP_A, me)
        swap(solved_b.at[k, me], back_swapped_b.at[k, me], k, BACK_SWAP_B, me)

    def combine_b(k, d):
        arrived(back_swapped_b.at[k, d], k, BACK_SWAP_B, d)
        combined_b[k, d] = back_swapped_b[k, d] + sign * solved_b[k, d]

    def own_back_b(k):
        return pltpu.make_async_copy(
            combined_b.at[k, me], out.at[0, :, columns(me, k, 1)], store_sem.at[k, n]
        )

    def back_relay(k):
        def body(i):
            d = target(i)
            combine_b(k, d)
            spread(combined_b.at[k, d], out.at[0, :, columns(me, k, 1)], k, BACK_SPREAD_B, d)
            s = source(i)
            arrived(back_a.at[k, s], k, BACK_SPREAD_A, s)
            swap(back_a.at[k, s], back_swapped_a.at[k, s], k, BACK_SWAP_A, s)

        def last():
            combine_b(k, me)
            own_back_b(k).start()

        return body, last

    def store_a(k, s):
        return pltpu.make_async_copy(
            combined_a.at[k, s], out.at[0, :, columns(s, k, 0)], store_sem.at[k, s]
        )

    def finish(k):
        def put(s, mine):
            arrived(back_swapped_a.at[k, s], k, BACK_SWAP_A, s)
            combined_a[k, s] = back_swapped_a[k, s] + sign * mine[k, s]
            store_a(k, s).start()

        put(me, solved_a)
        each(lambda i: put(source(i), back_a))

    def drain(k):
        def body(i):
            s = source(i)
            arrived(out.at[0, :, columns(s, k, 1)], k, BACK_SPREAD_B, s)
            d = target(i)
            for group in range(GROUPS):
                remote(landed_a.at[k, d], landed_a.at[k, d], k, group, d, d, partner).wait_send()
            store_a(k, s).wait()

        each(body)
        for group in (SWAP_A, SWAP_B, BACK_SWAP_A, BACK_SWAP_B):
            remote(landed_a.at[k, me], landed_a.at[k, me], k, group, me, me, partner).wait_send()
        store_a(k, me).wait()
        own_back_b(k).wait()

    forward_start(0)

    for copy in loads:
        copy.wait()

    def halve(t, carry):
        block = pl.ds(pl.multiple_of(t * TILE, TILE), TILE)
        for which in range(2):
            matrices[which, 0, block, :], matrices[which, 1, block, :] = split(staged[which, block, :])
        return carry

    lax.fori_loop(0, tiles, halve, 0)

    whole(forward_relay(0))
    forward_start(1)
    gather(0)
    compute(0, forward_relay(1))
    back_start(0)
    gather(1)
    compute(1, back_relay(0))
    back_start(1)
    whole(back_relay(1))
    finish(0)
    finish(1)
    for k in range(PAIRS):
        drain(k)


def shards(n, right_side, analysis, synthesis, negated_eigen, wave_square):
    rows, modes = right_side.shape[1:]
    height = analysis.shape[1]
    width = modes // n
    w = width // (2 * PAIRS)
    scratch_bytes = 4 * (modes * rows * 7 + height * height * 4 + height * w * 4)
    pieces = pltpu.VMEM((PAIRS, n, rows, w), jnp.float32)
    anywhere = pl.BlockSpec(memory_space=pl.ANY)
    vmem = pl.BlockSpec(memory_space=pltpu.VMEM)
    return pl.pallas_call(
        functools.partial(kernel, n),
        out_shape=jax.ShapeDtypeStruct(right_side.shape, jnp.float32),
        in_specs=[anywhere, anywhere, anywhere, vmem, vmem],
        out_specs=anywhere,
        scratch_shapes=[
            pltpu.VMEM((rows, modes), jnp.float32),
            pltpu.VMEM((2, height, height), jnp.float32),
            pltpu.VMEM((2, 2, height, height), jnp.bfloat16),
        ]
        + [pieces] * 5
        + [pltpu.VMEM((2, height, 2 * w), jnp.bfloat16)] * 2
        + [pieces] * 7
        + [
            pltpu.SemaphoreType.DMA((PAIRS * GROUPS, n)),
            pltpu.SemaphoreType.DMA((PAIRS * GROUPS, n)),
            pltpu.SemaphoreType.DMA((3,)),
            pltpu.SemaphoreType.DMA((PAIRS,)),
            pltpu.SemaphoreType.DMA((PAIRS, n + 1)),
        ],
        compiler_params=pltpu.CompilerParams(
            collective_id=0, has_side_effects=True, vmem_limit_bytes=scratch_bytes + 4 * 2**20
        ),
    )(right_side, analysis, synthesis, negated_eigen, wave_square[None])


def solution(mesh):
    return jax.shard_map(
        functools.partial(shards, mesh.shape["slab"]),
        mesh=mesh,
        in_specs=(
            P("mirror", "slab", "cols"),
            P("mirror", None, None),
            P("mirror", None, None),
            P("mirror", None),
            P(("cols", "slab")),
        ),
        out_specs=P("mirror", "slab", "cols"),
        check_vma=False,
    )
```

```python
import functools

import jax
import jax.numpy as jnp
from jax import lax
from jax.experimental import pallas as pl
from jax.experimental.pallas import tpu as pltpu
from jax.sharding import PartitionSpec as P

MESH = pl.DeviceIdType.MESH
PAIRS = 2
TILE = 256
SWAP_A, SPREAD_A, SPREAD_B, SWAP_B, BACK_SWAP_B, BACK_SPREAD_B, BACK_SPREAD_A, BACK_SWAP_A = range(8)
GROUPS = 8


def split(value):
    high = value.astype(jnp.bfloat16)
    return high, (value - high.astype(jnp.float32)).astype(jnp.bfloat16)


def kernel(
    n,
    field,
    analysis,
    synthesis,
    eigen_in,
    wave_in,
    out,
    own,
    staged,
    matrices,
    swapped_a,
    folded_a,
    landed_a,
    landed_b,
    swapped_b,
    right,
    scaled,
    solved_a,
    solved_b,
    back_a,
    back_swapped_a,
    back_swapped_b,
    combined_b,
    combined_a,
    eigen,
    wave,
    send_sem,
    recv_sem,
    load_sem,
    own_b_sem,
    store_sem,
):
    rows = field.shape[1]
    width = field.shape[2] // n
    w = width // (2 * PAIRS)
    height = analysis.shape[1]
    me = lax.axis_index("slab")
    parity = lax.axis_index("mirror")
    sign = (1 - 2 * parity).astype(jnp.float32)
    partner = {"mirror": 1 - parity}

    def offset(i):
        j = i // 2
        step = (j + 1) // 2
        far = n // 2 + (j % 2) * step + (1 - j % 2) * (n - step)
        near = (1 - j % 2) * (j // 2 + 1) + (j % 2) * (n - step)
        return lax.rem((1 - i % 2) * far + (i % 2) * near, n)

    def target(i):
        return lax.rem(me + offset(i), n)

    def source(i):
        return lax.rem(me + 2 * n - offset(i), n)

    def columns(d, k, b):
        return pl.ds(pl.multiple_of(d * width + (2 * k + b) * w, w), w)

    def remote(src, dst, k, group, sent, received, device):
        return pltpu.make_async_remote_copy(
            src_ref=src,
            dst_ref=dst,
            send_sem=send_sem.at[k * GROUPS + group, sent],
            recv_sem=recv_sem.at[k * GROUPS + group, received],
            device_id=device,
            device_id_type=MESH,
        )

    def swap(src, dst, k, group, d):
        remote(src, dst, k, group, d, d, partner).start()

    def spread(src, dst, k, group, d):
        remote(src, dst, k, group, d, me, {"slab": d}).start()

    def arrived(dst, k, group, s):
        remote(dst, dst, k, group, s, s, partner).wait_recv()

    def each(body, start=0, stop=n - 1):
        def step(i, carry):
            body(i)
            return carry

        lax.fori_loop(start, stop, step, 0)

    def whole(relay):
        body, last = relay
        each(body)
        last()

    loads = [
        pltpu.make_async_copy(field.at[0], own, load_sem.at[0]),
        pltpu.make_async_copy(analysis.at[0], staged.at[0], load_sem.at[1]),
        pltpu.make_async_copy(synthesis.at[0], staged.at[1], load_sem.at[2]),
        pltpu.make_async_copy(eigen_in, eigen, load_sem.at[3]),
        pltpu.make_async_copy(wave_in, wave, load_sem.at[4]),
    ]
    own_b = [
        pltpu.make_async_copy(field.at[0, :, columns(me, k, 1)], landed_b.at[k, me], own_b_sem.at[k])
        for k in range(PAIRS)
    ]
    for copy in loads + own_b:
        copy.start()

    barrier = pltpu.get_barrier_semaphore()

    def greet(i):
        pl.semaphore_signal(barrier, inc=1, device_id={"slab": target(i)}, device_id_type=MESH)

    each(greet)
    pl.semaphore_signal(barrier, inc=1, device_id=partner, device_id_type=MESH)
    pl.semaphore_wait(barrier, n)

    def forward_start(k):
        def body(i):
            d = target(i)
            swap(field.at[0, :, columns(d, k, 0)], swapped_a.at[k, d], k, SWAP_A, d)
            spread(field.at[0, :, columns(d, k, 1)], landed_b.at[k, me], k, SPREAD_B, d)

        each(body)
        swap(field.at[0, :, columns(me, k, 0)], swapped_a.at[k, me], k, SWAP_A, me)
        swap(field.at[0, :, columns(me, k, 1)], swapped_b.at[k, me], k, SWAP_B, me)

    def fold_a(k, d):
        arrived(swapped_a.at[k, d], k, SWAP_A, d)
        return (swapped_a[k, d] + sign * own[:, columns(d, k, 0)]) * 0.5

    def forward_relay(k):
        def body(i):
            d = target(i)
            folded_a[k, d] = fold_a(k, d)
            spread(folded_a.at[k, d], landed_a.at[k, me], k, SPREAD_A, d)
            s = source(i)
            arrived(landed_b.at[k, s], k, SPREAD_B, s)
            swap(landed_b.at[k, s], swapped_b.at[k, s], k, SWAP_B, s)

        def last():
            landed_a[k, me] = fold_a(k, me)
            own_b[k].wait()

        return body, last

    def gather(k):
        def put(s):
            block = pl.ds(pl.multiple_of(s * rows, rows), rows)
            right[0, block, :w], right[1, block, :w] = split(landed_a[k, s])
            arrived(swapped_b.at[k, s], k, SWAP_B, s)
            folded = (swapped_b[k, s] + sign * landed_b[k, s]) * 0.5
            right[0, block, w:], right[1, block, w:] = split(folded)

        put(me)

        def body(i):
            s = source(i)
            arrived(landed_a.at[k, s], k, SPREAD_A, s)
            put(s)

        each(body)

    tiles = height // TILE

    def product(which, operand, finish, beside):
        def step(t, carry):
            block = pl.ds(pl.multiple_of(t * TILE, TILE), TILE)
            high, low = matrices[which, 0, block, :], matrices[which, 1, block, :]
            dot = functools.partial(jnp.dot, preferred_element_type=jnp.float32)
            finish(t, block, dot(high, operand[0]) + (dot(high, operand[1]) + dot(low, operand[0])))
            at = which * tiles + t
            each(beside, at * (n - 1) // (2 * tiles), (at + 1) * (n - 1) // (2 * tiles))
            return carry

        lax.fori_loop(0, tiles, step, 0)

    def compute(k, relay):
        beside, last = relay

        def scale(t, block, total):
            shift = jnp.broadcast_to(eigen[0:1, block], (2 * w, TILE)).T
            value = total / (shift + wave[0:1, 2 * w * k : 2 * w * (k + 1)])
            scaled[0, block, :], scaled[1, block, :] = split(value)

        def keep(t, block, total):
            per = TILE // rows
            blocks = pl.ds(t * per, per)
            solved_a[k, blocks] = -total[:, :w].reshape(per, rows, w)
            solved_b[k, blocks] = -total[:, w:].reshape(per, rows, w)

        product(0, right, scale, beside)
        product(1, scaled, keep, beside)
        last()

    def back_start(k):
        def body(i):
            d = target(i)
            spread(solved_a.at[k, d], back_a.at[k, me], k, BACK_SPREAD_A, d)
            swap(solved_b.at[k, d], back_swapped_b.at[k, d], k, BACK_SWAP_B, d)

        each(body)
        swap(solved_a.at[k, me], back_swapped_a.at[k, me], k, BACK_SWAP_A, me)
        swap(solved_b.at[k, me], back_swapped_b.at[k, me], k, BACK_SWAP_B, me)

    def combine_b(k, d):
        arrived(back_swapped_b.at[k, d], k, BACK_SWAP_B, d)
        combined_b[k, d] = back_swapped_b[k, d] + sign * solved_b[k, d]

    def own_back_b(k):
        return pltpu.make_async_copy(
            combined_b.at[k, me], out.at[0, :, columns(me, k, 1)], store_sem.at[k, n]
        )

    def back_relay(k):
        def body(i):
            d = target(i)
            combine_b(k, d)
            spread(combined_b.at[k, d], out.at[0, :, columns(me, k, 1)], k, BACK_SPREAD_B, d)
            s = source(i)
            arrived(back_a.at[k, s], k, BACK_SPREAD_A, s)
            swap(back_a.at[k, s], back_swapped_a.at[k, s], k, BACK_SWAP_A, s)

        def last():
            combine_b(k, me)
            own_back_b(k).start()

        return body, last

    def store_a(k, s):
        return pltpu.make_async_copy(
            combined_a.at[k, s], out.at[0, :, columns(s, k, 0)], store_sem.at[k, s]
        )

    def finish(k):
        def put(s, mine):
            arrived(back_swapped_a.at[k, s], k, BACK_SWAP_A, s)
            combined_a[k, s] = back_swapped_a[k, s] + sign * mine[k, s]
            store_a(k, s).start()

        put(me, solved_a)
        each(lambda i: put(source(i), back_a))

    def drain(k):
        def body(i):
            s = source(i)
            arrived(out.at[0, :, columns(s, k, 1)], k, BACK_SPREAD_B, s)
            d = target(i)
            for group in range(GROUPS):
                remote(landed_a.at[k, d], landed_a.at[k, d], k, group, d, d, partner).wait_send()
            store_a(k, s).wait()

        each(body)
        for group in (SWAP_A, SWAP_B, BACK_SWAP_A, BACK_SWAP_B):
            remote(landed_a.at[k, me], landed_a.at[k, me], k, group, me, me, partner).wait_send()
        store_a(k, me).wait()
        own_back_b(k).wait()

    forward_start(0)

    for copy in loads:
        copy.wait()

    def halve(t, carry):
        block = pl.ds(pl.multiple_of(t * TILE, TILE), TILE)
        for which in range(2):
            matrices[which, 0, block, :], matrices[which, 1, block, :] = split(staged[which, block, :])
        return carry

    lax.fori_loop(0, tiles, halve, 0)

    whole(forward_relay(0))
    forward_start(1)
    gather(0)
    compute(0, forward_relay(1))
    back_start(0)
    gather(1)
    compute(1, back_relay(0))
    back_start(1)
    whole(back_relay(1))
    finish(0)
    finish(1)
    for k in range(PAIRS):
        drain(k)


def shards(n, right_side, analysis, synthesis, negated_eigen, wave_square):
    rows, modes = right_side.shape[1:]
    height = analysis.shape[1]
    width = modes // n
    w = width // (2 * PAIRS)
    scratch_bytes = 4 * (modes * rows * 7 + height * height * 4 + height * w * 4)
    pieces = pltpu.VMEM((PAIRS, n, rows, w), jnp.float32)
    anywhere = pl.BlockSpec(memory_space=pl.ANY)
    hbm = pl.BlockSpec(memory_space=pltpu.HBM)
    return pl.pallas_call(
        functools.partial(kernel, n),
        out_shape=jax.ShapeDtypeStruct(right_side.shape, jnp.float32),
        in_specs=[hbm] * 5,
        out_specs=anywhere,
        scratch_shapes=[
            pltpu.VMEM((rows, modes), jnp.float32),
            pltpu.VMEM((2, height, height), jnp.float32),
            pltpu.VMEM((2, 2, height, height), jnp.bfloat16),
        ]
        + [pieces] * 5
        + [pltpu.VMEM((2, height, 2 * w), jnp.bfloat16)] * 2
        + [pieces] * 7
        + [
            pltpu.VMEM((1, height), jnp.float32),
            pltpu.VMEM((1, width), jnp.float32),
            pltpu.SemaphoreType.DMA((PAIRS * GROUPS, n)),
            pltpu.SemaphoreType.DMA((PAIRS * GROUPS, n)),
            pltpu.SemaphoreType.DMA((5,)),
            pltpu.SemaphoreType.DMA((PAIRS,)),
            pltpu.SemaphoreType.DMA((PAIRS, n + 1)),
        ],
        compiler_params=pltpu.CompilerParams(
            collective_id=0, has_side_effects=True, vmem_limit_bytes=scratch_bytes + 4 * 2**20
        ),
    )(right_side, analysis, synthesis, negated_eigen, wave_square[None])


def solution(mesh):
    return jax.shard_map(
        functools.partial(shards, mesh.shape["slab"]),
        mesh=mesh,
        in_specs=(
            P("mirror", "slab", "cols"),
            P("mirror", None, None),
            P("mirror", None, None),
            P("mirror", None),
            P(("cols", "slab")),
        ),
        out_specs=P("mirror", "slab", "cols"),
        check_vma=False,
    )
```

```python
import functools

import jax
import jax.numpy as jnp
from jax import lax
from jax.experimental import pallas as pl
from jax.experimental.pallas import tpu as pltpu
from jax.sharding import PartitionSpec as P

MESH = pl.DeviceIdType.MESH
PAIRS = 2
TILE = 256
SWAP_A, SPREAD_A, SPREAD_B, SWAP_B, BACK_SWAP_B, BACK_SPREAD_B, BACK_SPREAD_A, BACK_SWAP_A = range(8)
GROUPS = 8


def split(value):
    high = value.astype(jnp.bfloat16)
    return high, (value - high.astype(jnp.float32)).astype(jnp.bfloat16)


def kernel(
    n,
    field,
    analysis,
    synthesis,
    eigen_in,
    wave_in,
    out,
    own,
    staged,
    matrices,
    swapped_a,
    folded_a,
    landed_a,
    landed_b,
    swapped_b,
    right,
    scaled,
    solved_a,
    solved_b,
    back_a,
    back_swapped_a,
    back_swapped_b,
    combined_b,
    combined_a,
    eigen,
    wave,
    send_sem,
    recv_sem,
    load_sem,
    own_b_sem,
    store_sem,
):
    rows = field.shape[1]
    width = field.shape[2] // n
    w = width // (2 * PAIRS)
    height = analysis.shape[1]
    me = lax.axis_index("slab")
    parity = lax.axis_index("mirror")
    sign = (1 - 2 * parity).astype(jnp.float32)
    partner = {"mirror": 1 - parity}

    def offset(i):
        half = (i + 1) // 2
        odd = i % 2
        return n // 2 + odd * half + (1 - odd) * (n - half)

    def target(i):
        return lax.rem(me + offset(i), n)

    def source(i):
        return lax.rem(me + 2 * n - offset(i), n)

    def columns(d, k, b):
        return pl.ds(pl.multiple_of(d * width + (2 * k + b) * w, w), w)

    def remote(src, dst, k, group, sent, received, device):
        return pltpu.make_async_remote_copy(
            src_ref=src,
            dst_ref=dst,
            send_sem=send_sem.at[k * GROUPS + group, sent],
            recv_sem=recv_sem.at[k * GROUPS + group, received],
            device_id=device,
            device_id_type=MESH,
        )

    def swap(src, dst, k, group, d):
        remote(src, dst, k, group, d, d, partner).start()

    def spread(src, dst, k, group, d):
        remote(src, dst, k, group, d, me, {"slab": d}).start()

    def arrived(dst, k, group, s):
        remote(dst, dst, k, group, s, s, partner).wait_recv()

    def each(body, start=0, stop=n - 1):
        def step(i, carry):
            body(i)
            return carry

        lax.fori_loop(start, stop, step, 0)

    def whole(relay):
        body, last = relay
        each(body)
        last()

    loads = [
        pltpu.make_async_copy(field.at[0], own, load_sem.at[0]),
        pltpu.make_async_copy(analysis.at[0], staged.at[0], load_sem.at[1]),
        pltpu.make_async_copy(synthesis.at[0], staged.at[1], load_sem.at[2]),
        pltpu.make_async_copy(eigen_in, eigen, load_sem.at[3]),
        pltpu.make_async_copy(wave_in, wave, load_sem.at[4]),
    ]
    own_b = [
        pltpu.make_async_copy(field.at[0, :, columns(me, k, 1)], landed_b.at[k, me], own_b_sem.at[k])
        for k in range(PAIRS)
    ]
    barrier = pltpu.get_barrier_semaphore()

    def greet(i):
        pl.semaphore_signal(barrier, inc=1, device_id={"slab": target(i)}, device_id_type=MESH)

    each(greet)
    pl.semaphore_signal(barrier, inc=1, device_id=partner, device_id_type=MESH)
    pl.semaphore_wait(barrier, n)

    def forward_start(k):
        def body(i):
            d = target(i)
            swap(field.at[0, :, columns(d, k, 0)], swapped_a.at[k, d], k, SWAP_A, d)
            spread(field.at[0, :, columns(d, k, 1)], landed_b.at[k, me], k, SPREAD_B, d)

        each(body)
        swap(field.at[0, :, columns(me, k, 0)], swapped_a.at[k, me], k, SWAP_A, me)
        swap(field.at[0, :, columns(me, k, 1)], swapped_b.at[k, me], k, SWAP_B, me)

    def fold_a(k, d):
        arrived(swapped_a.at[k, d], k, SWAP_A, d)
        return (swapped_a[k, d] + sign * own[:, columns(d, k, 0)]) * 0.5

    def forward_relay(k):
        def body(i):
            d = target(i)
            folded_a[k, d] = fold_a(k, d)
            spread(folded_a.at[k, d], landed_a.at[k, me], k, SPREAD_A, d)
            s = source(i)
            arrived(landed_b.at[k, s], k, SPREAD_B, s)
            swap(landed_b.at[k, s], swapped_b.at[k, s], k, SWAP_B, s)

        def last():
            landed_a[k, me] = fold_a(k, me)
            own_b[k].wait()

        return body, last

    def gather(k):
        def put(s):
            block = pl.ds(pl.multiple_of(s * rows, rows), rows)
            right[0, block, :w], right[1, block, :w] = split(landed_a[k, s])
            arrived(swapped_b.at[k, s], k, SWAP_B, s)
            folded = (swapped_b[k, s] + sign * landed_b[k, s]) * 0.5
            right[0, block, w:], right[1, block, w:] = split(folded)

        put(me)

        def body(i):
            s = source(i)
            arrived(landed_a.at[k, s], k, SPREAD_A, s)
            put(s)

        each(body)

    tiles = height // TILE

    def product(which, operand, finish, beside):
        def step(t, carry):
            block = pl.ds(pl.multiple_of(t * TILE, TILE), TILE)
            high, low = matrices[which, 0, block, :], matrices[which, 1, block, :]
            dot = functools.partial(jnp.dot, preferred_element_type=jnp.float32)
            finish(t, block, dot(high, operand[0]) + (dot(high, operand[1]) + dot(low, operand[0])))
            at = which * tiles + t
            each(beside, at * (n - 1) // (2 * tiles), (at + 1) * (n - 1) // (2 * tiles))
            return carry

        lax.fori_loop(0, tiles, step, 0)

    def compute(k, relay):
        beside, last = relay

        def scale(t, block, total):
            shift = jnp.broadcast_to(eigen[0:1, block], (2 * w, TILE)).T
            value = total / (shift + wave[0:1, 2 * w * k : 2 * w * (k + 1)])
            scaled[0, block, :], scaled[1, block, :] = split(value)

        def keep(t, block, total):
            per = TILE // rows
            blocks = pl.ds(t * per, per)
            solved_a[k, blocks] = -total[:, :w].reshape(per, rows, w)
            solved_b[k, blocks] = -total[:, w:].reshape(per, rows, w)

        product(0, right, scale, beside)
        product(1, scaled, keep, beside)
        last()

    def back_start(k):
        def body(i):
            d = target(i)
            spread(solved_a.at[k, d], back_a.at[k, me], k, BACK_SPREAD_A, d)
            swap(solved_b.at[k, d], back_swapped_b.at[k, d], k, BACK_SWAP_B, d)

        each(body)
        swap(solved_a.at[k, me], back_swapped_a.at[k, me], k, BACK_SWAP_A, me)
        swap(solved_b.at[k, me], back_swapped_b.at[k, me], k, BACK_SWAP_B, me)

    def combine_b(k, d):
        arrived(back_swapped_b.at[k, d], k, BACK_SWAP_B, d)
        combined_b[k, d] = back_swapped_b[k, d] + sign * solved_b[k, d]

    def own_back_b(k):
        return pltpu.make_async_copy(
            combined_b.at[k, me], out.at[0, :, columns(me, k, 1)], store_sem.at[k, n]
        )

    def back_relay(k):
        def body(i):
            d = target(i)
            combine_b(k, d)
            spread(combined_b.at[k, d], out.at[0, :, columns(me, k, 1)], k, BACK_SPREAD_B, d)
            s = source(i)
            arrived(back_a.at[k, s], k, BACK_SPREAD_A, s)
            swap(back_a.at[k, s], back_swapped_a.at[k, s], k, BACK_SWAP_A, s)

        def last():
            combine_b(k, me)
            own_back_b(k).start()

        return body, last

    def store_a(k, s):
        return pltpu.make_async_copy(
            combined_a.at[k, s], out.at[0, :, columns(s, k, 0)], store_sem.at[k, s]
        )

    def finish(k):
        def put(s, mine):
            arrived(back_swapped_a.at[k, s], k, BACK_SWAP_A, s)
            combined_a[k, s] = back_swapped_a[k, s] + sign * mine[k, s]
            store_a(k, s).start()

        put(me, solved_a)
        each(lambda i: put(source(i), back_a))

    def drain(k):
        def body(i):
            s = source(i)
            arrived(out.at[0, :, columns(s, k, 1)], k, BACK_SPREAD_B, s)
            d = target(i)
            for group in range(GROUPS):
                remote(landed_a.at[k, d], landed_a.at[k, d], k, group, d, d, partner).wait_send()
            store_a(k, s).wait()

        each(body)
        for group in (SWAP_A, SWAP_B, BACK_SWAP_A, BACK_SWAP_B):
            remote(landed_a.at[k, me], landed_a.at[k, me], k, group, me, me, partner).wait_send()
        store_a(k, me).wait()
        own_back_b(k).wait()

    forward_start(0)
    for copy in loads + own_b:
        copy.start()

    def halve(t, carry):
        block = pl.ds(pl.multiple_of(t * TILE, TILE), TILE)
        for which in range(2):
            matrices[which, 0, block, :], matrices[which, 1, block, :] = split(staged[which, block, :])
        return carry

    loads[0].wait()
    whole(forward_relay(0))
    forward_start(1)
    for copy in loads[1:]:
        copy.wait()
    lax.fori_loop(0, tiles, halve, 0)
    gather(0)
    compute(0, forward_relay(1))
    back_start(0)
    gather(1)
    compute(1, back_relay(0))
    back_start(1)
    whole(back_relay(1))
    finish(0)
    finish(1)
    for k in range(PAIRS):
        drain(k)


def shards(n, right_side, analysis, synthesis, negated_eigen, wave_square):
    rows, modes = right_side.shape[1:]
    height = analysis.shape[1]
    width = modes // n
    w = width // (2 * PAIRS)
    scratch_bytes = 4 * (modes * rows * 7 + height * height * 4 + height * w * 4)
    pieces = pltpu.VMEM((PAIRS, n, rows, w), jnp.float32)
    anywhere = pl.BlockSpec(memory_space=pl.ANY)
    hbm = pl.BlockSpec(memory_space=pltpu.HBM)
    return pl.pallas_call(
        functools.partial(kernel, n),
        out_shape=jax.ShapeDtypeStruct(right_side.shape, jnp.float32),
        in_specs=[hbm] * 5,
        out_specs=anywhere,
        scratch_shapes=[
            pltpu.VMEM((rows, modes), jnp.float32),
            pltpu.VMEM((2, height, height), jnp.float32),
            pltpu.VMEM((2, 2, height, height), jnp.bfloat16),
        ]
        + [pieces] * 5
        + [pltpu.VMEM((2, height, 2 * w), jnp.bfloat16)] * 2
        + [pieces] * 7
        + [
            pltpu.VMEM((1, height), jnp.float32),
            pltpu.VMEM((1, width), jnp.float32),
            pltpu.SemaphoreType.DMA((PAIRS * GROUPS, n)),
            pltpu.SemaphoreType.DMA((PAIRS * GROUPS, n)),
            pltpu.SemaphoreType.DMA((5,)),
            pltpu.SemaphoreType.DMA((PAIRS,)),
            pltpu.SemaphoreType.DMA((PAIRS, n + 1)),
        ],
        compiler_params=pltpu.CompilerParams(
            collective_id=0, has_side_effects=True, vmem_limit_bytes=scratch_bytes + 4 * 2**20
        ),
    )(*(
        pltpu.with_memory_space_constraint(value, pltpu.HBM)
        for value in (right_side, analysis, synthesis, negated_eigen, wave_square[None])
    ))


def solution(mesh):
    return jax.shard_map(
        functools.partial(shards, mesh.shape["slab"]),
        mesh=mesh,
        in_specs=(
            P("mirror", "slab", "cols"),
            P("mirror", None, None),
            P("mirror", None, None),
            P("mirror", None),
            P(("cols", "slab")),
        ),
        out_specs=P("mirror", "slab", "cols"),
        check_vma=False,
    )
```

```python
import functools

import jax
import jax.numpy as jnp
from jax import lax
from jax.experimental import pallas as pl
from jax.experimental.pallas import tpu as pltpu
from jax.sharding import PartitionSpec as P

MESH = pl.DeviceIdType.MESH
PAIRS = 2
TILE = 256
SWAP_A, SPREAD_A, SPREAD_B, SWAP_B, BACK_SWAP_B, BACK_SPREAD_B, BACK_SPREAD_A, BACK_SWAP_A = range(8)
GROUPS = 8


def split(value):
    high = value.astype(jnp.bfloat16)
    return high, (value - high.astype(jnp.float32)).astype(jnp.bfloat16)


def kernel(
    n,
    field,
    analysis,
    synthesis,
    eigen_in,
    wave_in,
    out,
    own,
    staged,
    matrices,
    swapped_a,
    folded_a,
    landed_a,
    landed_b,
    swapped_b,
    right,
    scaled,
    solved_a,
    solved_b,
    back_a,
    back_swapped_a,
    back_swapped_b,
    combined_b,
    combined_a,
    eigen,
    wave,
    send_sem,
    recv_sem,
    load_sem,
    own_b_sem,
    store_sem,
):
    rows = field.shape[1]
    width = field.shape[2] // n
    w = width // (2 * PAIRS)
    height = analysis.shape[1]
    me = lax.axis_index("slab")
    parity = lax.axis_index("mirror")
    sign = (1 - 2 * parity).astype(jnp.float32)
    partner = {"mirror": 1 - parity}

    def offset(i):
        half = (i + 1) // 2
        odd = i % 2
        return n // 2 + odd * half + (1 - odd) * (n - half)

    def target(i):
        return lax.rem(me + offset(i), n)

    def source(i):
        return lax.rem(me + 2 * n - offset(i), n)

    def columns(d, k, b):
        return pl.ds(pl.multiple_of(d * width + (2 * k + b) * w, w), w)

    def remote(src, dst, k, group, sent, received, device):
        return pltpu.make_async_remote_copy(
            src_ref=src,
            dst_ref=dst,
            send_sem=send_sem.at[k * GROUPS + group, sent],
            recv_sem=recv_sem.at[k * GROUPS + group, received],
            device_id=device,
            device_id_type=MESH,
        )

    def swap(src, dst, k, group, d):
        remote(src, dst, k, group, d, d, partner).start()

    def spread(src, dst, k, group, d):
        remote(src, dst, k, group, d, me, {"slab": d}).start()

    def arrived(dst, k, group, s):
        remote(dst, dst, k, group, s, s, partner).wait_recv()

    def each(body, start=0, stop=n - 1):
        def step(i, carry):
            body(i)
            return carry

        lax.fori_loop(start, stop, step, 0)

    def whole(relay):
        body, last = relay
        each(body)
        last()

    loads = [
        pltpu.make_async_copy(field.at[0], own, load_sem.at[0]),
        pltpu.make_async_copy(analysis.at[0], staged.at[0], load_sem.at[1]),
        pltpu.make_async_copy(synthesis.at[0], staged.at[1], load_sem.at[2]),
        pltpu.make_async_copy(eigen_in, eigen, load_sem.at[3]),
        pltpu.make_async_copy(wave_in, wave, load_sem.at[4]),
    ]
    own_b = [
        pltpu.make_async_copy(field.at[0, :, columns(me, k, 1)], landed_b.at[k, me], own_b_sem.at[k])
        for k in range(PAIRS)
    ]
    barrier = pltpu.get_barrier_semaphore()

    def greet(i):
        pl.semaphore_signal(barrier, inc=1, device_id={"slab": target(i)}, device_id_type=MESH)

    each(greet)
    pl.semaphore_signal(barrier, inc=1, device_id=partner, device_id_type=MESH)
    pl.semaphore_wait(barrier, n)

    def forward_start(k):
        def body(i):
            d = target(i)
            swap(field.at[0, :, columns(d, k, 0)], swapped_a.at[k, d], k, SWAP_A, d)
            spread(field.at[0, :, columns(d, k, 1)], landed_b.at[k, me], k, SPREAD_B, d)

        each(body)
        swap(field.at[0, :, columns(me, k, 0)], swapped_a.at[k, me], k, SWAP_A, me)
        swap(field.at[0, :, columns(me, k, 1)], swapped_b.at[k, me], k, SWAP_B, me)

    def fold_a(k, d):
        arrived(swapped_a.at[k, d], k, SWAP_A, d)
        return (swapped_a[k, d] + sign * own[:, columns(d, k, 0)]) * 0.5

    def forward_relay(k):
        def body(i):
            d = target(i)
            folded_a[k, d] = fold_a(k, d)
            spread(folded_a.at[k, d], landed_a.at[k, me], k, SPREAD_A, d)
            s = source(n - 2 - i)
            arrived(landed_b.at[k, s], k, SPREAD_B, s)
            swap(landed_b.at[k, s], swapped_b.at[k, s], k, SWAP_B, s)

        def last():
            landed_a[k, me] = fold_a(k, me)
            own_b[k].wait()

        return body, last

    def gather(k):
        def put(s):
            block = pl.ds(pl.multiple_of(s * rows, rows), rows)
            right[0, block, :w], right[1, block, :w] = split(landed_a[k, s])
            arrived(swapped_b.at[k, s], k, SWAP_B, s)
            folded = (swapped_b[k, s] + sign * landed_b[k, s]) * 0.5
            right[0, block, w:], right[1, block, w:] = split(folded)

        put(me)

        def body(i):
            s = source(i)
            arrived(landed_a.at[k, s], k, SPREAD_A, s)
            put(s)

        each(body)

    tiles = height // TILE

    def product(which, operand, finish, beside):
        def step(t, carry):
            block = pl.ds(pl.multiple_of(t * TILE, TILE), TILE)
            high, low = matrices[which, 0, block, :], matrices[which, 1, block, :]
            dot = functools.partial(jnp.dot, preferred_element_type=jnp.float32)
            finish(t, block, dot(high, operand[0]) + (dot(high, operand[1]) + dot(low, operand[0])))
            at = which * tiles + t
            each(beside, at * (n - 1) // (2 * tiles), (at + 1) * (n - 1) // (2 * tiles))
            return carry

        lax.fori_loop(0, tiles, step, 0)

    def compute(k, relay):
        beside, last = relay

        def scale(t, block, total):
            shift = jnp.broadcast_to(eigen[0:1, block], (2 * w, TILE)).T
            value = total / (shift + wave[0:1, 2 * w * k : 2 * w * (k + 1)])
            scaled[0, block, :], scaled[1, block, :] = split(value)

        def keep(t, block, total):
            per = TILE // rows
            blocks = pl.ds(t * per, per)
            solved_a[k, blocks] = -total[:, :w].reshape(per, rows, w)
            solved_b[k, blocks] = -total[:, w:].reshape(per, rows, w)

        product(0, right, scale, beside)
        product(1, scaled, keep, beside)
        last()

    def back_start(k):
        def body(i):
            d = target(i)
            spread(solved_a.at[k, d], back_a.at[k, me], k, BACK_SPREAD_A, d)
            swap(solved_b.at[k, d], back_swapped_b.at[k, d], k, BACK_SWAP_B, d)

        each(body)
        swap(solved_a.at[k, me], back_swapped_a.at[k, me], k, BACK_SWAP_A, me)
        swap(solved_b.at[k, me], back_swapped_b.at[k, me], k, BACK_SWAP_B, me)

    def combine_b(k, d):
        arrived(back_swapped_b.at[k, d], k, BACK_SWAP_B, d)
        combined_b[k, d] = back_swapped_b[k, d] + sign * solved_b[k, d]

    def own_back_b(k):
        return pltpu.make_async_copy(
            combined_b.at[k, me], out.at[0, :, columns(me, k, 1)], store_sem.at[k, n]
        )

    def back_relay(k):
        def body(i):
            d = target(i)
            combine_b(k, d)
            spread(combined_b.at[k, d], out.at[0, :, columns(me, k, 1)], k, BACK_SPREAD_B, d)
            s = source(n - 2 - i)
            arrived(back_a.at[k, s], k, BACK_SPREAD_A, s)
            swap(back_a.at[k, s], back_swapped_a.at[k, s], k, BACK_SWAP_A, s)

        def last():
            combine_b(k, me)
            own_back_b(k).start()

        return body, last

    def store_a(k, s):
        return pltpu.make_async_copy(
            combined_a.at[k, s], out.at[0, :, columns(s, k, 0)], store_sem.at[k, s]
        )

    def finish(k):
        def put(s, mine):
            arrived(back_swapped_a.at[k, s], k, BACK_SWAP_A, s)
            combined_a[k, s] = back_swapped_a[k, s] + sign * mine[k, s]
            store_a(k, s).start()

        put(me, solved_a)
        each(lambda i: put(source(i), back_a))

    def drain(k):
        def body(i):
            s = source(i)
            arrived(out.at[0, :, columns(s, k, 1)], k, BACK_SPREAD_B, s)
            d = target(i)
            for group in range(GROUPS):
                remote(landed_a.at[k, d], landed_a.at[k, d], k, group, d, d, partner).wait_send()
            store_a(k, s).wait()

        each(body)
        for group in (SWAP_A, SWAP_B, BACK_SWAP_A, BACK_SWAP_B):
            remote(landed_a.at[k, me], landed_a.at[k, me], k, group, me, me, partner).wait_send()
        store_a(k, me).wait()
        own_back_b(k).wait()

    forward_start(0)
    for copy in loads + own_b:
        copy.start()

    def halve(t, carry):
        block = pl.ds(pl.multiple_of(t * TILE, TILE), TILE)
        for which in range(2):
            matrices[which, 0, block, :], matrices[which, 1, block, :] = split(staged[which, block, :])
        return carry

    loads[0].wait()
    relay, last = forward_relay(0)
    each(relay, 0, n // 2)
    forward_start(1)
    each(relay, n // 2)
    last()
    for copy in loads[1:]:
        copy.wait()
    lax.fori_loop(0, tiles, halve, 0)
    gather(0)
    compute(0, forward_relay(1))
    back_start(0)
    gather(1)
    compute(1, back_relay(0))
    back_start(1)
    whole(back_relay(1))
    finish(0)
    finish(1)
    for k in range(PAIRS):
        drain(k)


def shards(n, right_side, analysis, synthesis, negated_eigen, wave_square):
    rows, modes = right_side.shape[1:]
    height = analysis.shape[1]
    width = modes // n
    w = width // (2 * PAIRS)
    scratch_bytes = 4 * (modes * rows * 7 + height * height * 4 + height * w * 4)
    pieces = pltpu.VMEM((PAIRS, n, rows, w), jnp.float32)
    anywhere = pl.BlockSpec(memory_space=pl.ANY)
    hbm = pl.BlockSpec(memory_space=pltpu.HBM)
    return pl.pallas_call(
        functools.partial(kernel, n),
        out_shape=jax.ShapeDtypeStruct(right_side.shape, jnp.float32),
        in_specs=[hbm] * 5,
        out_specs=anywhere,
        scratch_shapes=[
            pltpu.VMEM((rows, modes), jnp.float32),
            pltpu.VMEM((2, height, height), jnp.float32),
            pltpu.VMEM((2, 2, height, height), jnp.bfloat16),
        ]
        + [pieces] * 5
        + [pltpu.VMEM((2, height, 2 * w), jnp.bfloat16)] * 2
        + [pieces] * 7
        + [
            pltpu.VMEM((1, height), jnp.float32),
            pltpu.VMEM((1, width), jnp.float32),
            pltpu.SemaphoreType.DMA((PAIRS * GROUPS, n)),
            pltpu.SemaphoreType.DMA((PAIRS * GROUPS, n)),
            pltpu.SemaphoreType.DMA((5,)),
            pltpu.SemaphoreType.DMA((PAIRS,)),
            pltpu.SemaphoreType.DMA((PAIRS, n + 1)),
        ],
        compiler_params=pltpu.CompilerParams(
            collective_id=0, has_side_effects=True, vmem_limit_bytes=scratch_bytes + 4 * 2**20
        ),
    )(*(
        pltpu.with_memory_space_constraint(value, pltpu.HBM)
        for value in (right_side, analysis, synthesis, negated_eigen, wave_square[None])
    ))


def solution(mesh):
    return jax.shard_map(
        functools.partial(shards, mesh.shape["slab"]),
        mesh=mesh,
        in_specs=(
            P("mirror", "slab", "cols"),
            P("mirror", None, None),
            P("mirror", None, None),
            P("mirror", None),
            P(("cols", "slab")),
        ),
        out_specs=P("mirror", "slab", "cols"),
        check_vma=False,
    )
```

```python
import functools

import jax
import jax.numpy as jnp
from jax import lax
from jax.experimental import pallas as pl
from jax.experimental.pallas import tpu as pltpu
from jax.sharding import PartitionSpec as P

MESH = pl.DeviceIdType.MESH
PAIRS = 2
TILE = 256
SWAP_A, SPREAD_A, SPREAD_B, SWAP_B, BACK_SWAP_B, BACK_SPREAD_B, BACK_SPREAD_A, BACK_SWAP_A = range(8)
GROUPS = 8


def split(value):
    high = value.astype(jnp.bfloat16)
    return high, (value - high.astype(jnp.float32)).astype(jnp.bfloat16)


def kernel(
    n,
    field,
    analysis,
    synthesis,
    eigen_in,
    wave_in,
    out,
    own,
    staged,
    matrices,
    swapped_a,
    folded_a,
    landed_a,
    landed_b,
    swapped_b,
    right,
    scaled,
    solved_a,
    solved_b,
    back_a,
    back_swapped_a,
    back_swapped_b,
    combined_b,
    combined_a,
    eigen,
    wave,
    send_sem,
    recv_sem,
    load_sem,
    own_b_sem,
    store_sem,
):
    rows = field.shape[1]
    width = field.shape[2] // n
    w = width // (2 * PAIRS)
    height = analysis.shape[1]
    me = lax.axis_index("slab")
    parity = lax.axis_index("mirror")
    sign = (1 - 2 * parity).astype(jnp.float32)
    partner = {"mirror": 1 - parity}

    def offset(i):
        half = (i + 1) // 2
        odd = i % 2
        return n // 2 + odd * half + (1 - odd) * (n - half)

    def target(i):
        return lax.rem(me + offset(i), n)

    def source(i):
        return lax.rem(me + 2 * n - offset(i), n)

    def columns(d, k, b):
        return pl.ds(pl.multiple_of(d * width + (2 * k + b) * w, w), w)

    def remote(src, dst, k, group, received, device):
        return pltpu.make_async_remote_copy(
            src_ref=src,
            dst_ref=dst,
            send_sem=send_sem.at[k * GROUPS + group],
            recv_sem=recv_sem.at[k * GROUPS + group, received],
            device_id=device,
            device_id_type=MESH,
        )

    def swap(src, dst, k, group, d):
        remote(src, dst, k, group, d, partner).start()

    def spread(src, dst, k, group, d):
        remote(src, dst, k, group, me, {"slab": d}).start()

    def arrived(dst, k, group, s):
        remote(dst, dst, k, group, s, partner).wait_recv()

    def each(body, start=0, stop=n - 1):
        def step(i, carry):
            body(i)
            return carry

        lax.fori_loop(start, stop, step, 0)

    def whole(relay):
        body, last = relay
        each(body)
        last()

    loads = [
        pltpu.make_async_copy(field.at[0], own, load_sem.at[0]),
        pltpu.make_async_copy(analysis.at[0], staged.at[0], load_sem.at[1]),
        pltpu.make_async_copy(synthesis.at[0], staged.at[1], load_sem.at[2]),
        pltpu.make_async_copy(eigen_in, eigen, load_sem.at[3]),
        pltpu.make_async_copy(wave_in, wave, load_sem.at[4]),
    ]
    own_b = [
        pltpu.make_async_copy(field.at[0, :, columns(me, k, 1)], landed_b.at[k, me], own_b_sem.at[k])
        for k in range(PAIRS)
    ]
    barrier = pltpu.get_barrier_semaphore()

    def greet(i):
        pl.semaphore_signal(barrier, inc=1, device_id={"slab": target(i)}, device_id_type=MESH)

    each(greet)
    pl.semaphore_signal(barrier, inc=1, device_id=partner, device_id_type=MESH)
    pl.semaphore_wait(barrier, n)

    def forward_start(k):
        def body(i):
            d = target(i)
            swap(field.at[0, :, columns(d, k, 0)], swapped_a.at[k, d], k, SWAP_A, d)
            spread(field.at[0, :, columns(d, k, 1)], landed_b.at[k, me], k, SPREAD_B, d)

        each(body)
        swap(field.at[0, :, columns(me, k, 0)], swapped_a.at[k, me], k, SWAP_A, me)
        swap(field.at[0, :, columns(me, k, 1)], swapped_b.at[k, me], k, SWAP_B, me)

    def fold_a(k, d):
        arrived(swapped_a.at[k, d], k, SWAP_A, d)
        return (swapped_a[k, d] + sign * own[:, columns(d, k, 0)]) * 0.5

    def forward_relay(k):
        def body(i):
            d = target(i)
            folded_a[k, d] = fold_a(k, d)
            spread(folded_a.at[k, d], landed_a.at[k, me], k, SPREAD_A, d)
            s = source(i)
            arrived(landed_b.at[k, s], k, SPREAD_B, s)
            swap(landed_b.at[k, s], swapped_b.at[k, s], k, SWAP_B, s)

        def last():
            landed_a[k, me] = fold_a(k, me)
            own_b[k].wait()

        return body, last

    def gather(k):
        def put(s):
            block = pl.ds(pl.multiple_of(s * rows, rows), rows)
            right[0, block, :w], right[1, block, :w] = split(landed_a[k, s])
            arrived(swapped_b.at[k, s], k, SWAP_B, s)
            folded = (swapped_b[k, s] + sign * landed_b[k, s]) * 0.5
            right[0, block, w:], right[1, block, w:] = split(folded)

        put(me)

        def body(i):
            s = source(i)
            arrived(landed_a.at[k, s], k, SPREAD_A, s)
            put(s)

        each(body)

    tiles = height // TILE

    def product(which, operand, finish, beside):
        def step(t, carry):
            block = pl.ds(pl.multiple_of(t * TILE, TILE), TILE)
            high, low = matrices[which, 0, block, :], matrices[which, 1, block, :]
            dot = functools.partial(jnp.dot, preferred_element_type=jnp.float32)
            finish(t, block, dot(high, operand[0]) + (dot(high, operand[1]) + dot(low, operand[0])))
            at = which * tiles + t
            each(beside, at * (n - 1) // (2 * tiles), (at + 1) * (n - 1) // (2 * tiles))
            return carry

        lax.fori_loop(0, tiles, step, 0)

    def compute(k, relay):
        beside, last = relay

        def scale(t, block, total):
            shift = jnp.broadcast_to(eigen[0:1, block], (2 * w, TILE)).T
            value = total / (shift + wave[0:1, 2 * w * k : 2 * w * (k + 1)])
            scaled[0, block, :], scaled[1, block, :] = split(value)

        def keep(t, block, total):
            per = TILE // rows
            blocks = pl.ds(t * per, per)
            solved_a[k, blocks] = -total[:, :w].reshape(per, rows, w)
            solved_b[k, blocks] = -total[:, w:].reshape(per, rows, w)

        product(0, right, scale, beside)
        product(1, scaled, keep, beside)
        last()

    def back_start(k):
        def body(i):
            d = target(i)
            spread(solved_a.at[k, d], back_a.at[k, me], k, BACK_SPREAD_A, d)
            swap(solved_b.at[k, d], back_swapped_b.at[k, d], k, BACK_SWAP_B, d)

        each(body)
        swap(solved_a.at[k, me], back_swapped_a.at[k, me], k, BACK_SWAP_A, me)
        swap(solved_b.at[k, me], back_swapped_b.at[k, me], k, BACK_SWAP_B, me)

    def combine_b(k, d):
        arrived(back_swapped_b.at[k, d], k, BACK_SWAP_B, d)
        combined_b[k, d] = back_swapped_b[k, d] + sign * solved_b[k, d]

    def own_back_b(k):
        return pltpu.make_async_copy(
            combined_b.at[k, me], out.at[0, :, columns(me, k, 1)], store_sem.at[k, n]
        )

    def back_relay(k):
        def body(i):
            d = target(i)
            combine_b(k, d)
            spread(combined_b.at[k, d], out.at[0, :, columns(me, k, 1)], k, BACK_SPREAD_B, d)
            s = source(i)
            arrived(back_a.at[k, s], k, BACK_SPREAD_A, s)
            swap(back_a.at[k, s], back_swapped_a.at[k, s], k, BACK_SWAP_A, s)

        def last():
            combine_b(k, me)
            own_back_b(k).start()

        return body, last

    def store_a(k, s):
        return pltpu.make_async_copy(
            combined_a.at[k, s], out.at[0, :, columns(s, k, 0)], store_sem.at[k, s]
        )

    def finish(k):
        def put(s, mine):
            arrived(back_swapped_a.at[k, s], k, BACK_SWAP_A, s)
            combined_a[k, s] = back_swapped_a[k, s] + sign * mine[k, s]
            store_a(k, s).start()

        put(me, solved_a)
        each(lambda i: put(source(i), back_a))

    def sent(k, *groups):
        for group in groups:
            swaps = group in (SWAP_A, SWAP_B, BACK_SWAP_A, BACK_SWAP_B)
            pieces = landed_a.at[k, pl.ds(0, n if swaps else n - 1)]
            remote(pieces, pieces, k, group, 0, partner).wait_send()

    def drain(k):
        def body(i):
            s = source(i)
            arrived(out.at[0, :, columns(s, k, 1)], k, BACK_SPREAD_B, s)
            store_a(k, s).wait()

        each(body)
        store_a(k, me).wait()
        own_back_b(k).wait()

    forward_start(0)
    for copy in loads + own_b:
        copy.start()

    def halve(t, carry):
        block = pl.ds(pl.multiple_of(t * TILE, TILE), TILE)
        for which in range(2):
            matrices[which, 0, block, :], matrices[which, 1, block, :] = split(staged[which, block, :])
        return carry

    loads[0].wait()
    whole(forward_relay(0))
    forward_start(1)
    for copy in loads[1:]:
        copy.wait()
    lax.fori_loop(0, tiles, halve, 0)
    gather(0)
    compute(0, forward_relay(1))
    back_start(0)
    gather(1)
    compute(1, back_relay(0))
    back_start(1)
    for k in range(PAIRS):
        sent(k, SWAP_A, SPREAD_A, SPREAD_B, SWAP_B)
    whole(back_relay(1))
    finish(0)
    sent(0, BACK_SWAP_B, BACK_SPREAD_B, BACK_SPREAD_A, BACK_SWAP_A)
    drain(0)
    sent(1, BACK_SWAP_B, BACK_SPREAD_A)
    finish(1)
    drain(1)
    sent(1, BACK_SPREAD_B, BACK_SWAP_A)


def shards(n, right_side, analysis, synthesis, negated_eigen, wave_square):
    rows, modes = right_side.shape[1:]
    height = analysis.shape[1]
    width = modes // n
    w = width // (2 * PAIRS)
    scratch_bytes = 4 * (modes * rows * 7 + height * height * 4 + height * w * 4)
    pieces = pltpu.VMEM((PAIRS, n, rows, w), jnp.float32)
    anywhere = pl.BlockSpec(memory_space=pl.ANY)
    hbm = pl.BlockSpec(memory_space=pltpu.HBM)
    return pl.pallas_call(
        functools.partial(kernel, n),
        out_shape=jax.ShapeDtypeStruct(right_side.shape, jnp.float32),
        in_specs=[hbm] * 5,
        out_specs=anywhere,
        scratch_shapes=[
            pltpu.VMEM((rows, modes), jnp.float32),
            pltpu.VMEM((2, height, height), jnp.float32),
            pltpu.VMEM((2, 2, height, height), jnp.bfloat16),
        ]
        + [pieces] * 5
        + [pltpu.VMEM((2, height, 2 * w), jnp.bfloat16)] * 2
        + [pieces] * 7
        + [
            pltpu.VMEM((1, height), jnp.float32),
            pltpu.VMEM((1, width), jnp.float32),
            pltpu.SemaphoreType.DMA((PAIRS * GROUPS,)),
            pltpu.SemaphoreType.DMA((PAIRS * GROUPS, n)),
            pltpu.SemaphoreType.DMA((5,)),
            pltpu.SemaphoreType.DMA((PAIRS,)),
            pltpu.SemaphoreType.DMA((PAIRS, n + 1)),
        ],
        compiler_params=pltpu.CompilerParams(
            collective_id=0, has_side_effects=True, vmem_limit_bytes=scratch_bytes + 4 * 2**20
        ),
    )(*(
        pltpu.with_memory_space_constraint(value, pltpu.HBM)
        for value in (right_side, analysis, synthesis, negated_eigen, wave_square[None])
    ))


def solution(mesh):
    return jax.shard_map(
        functools.partial(shards, mesh.shape["slab"]),
        mesh=mesh,
        in_specs=(
            P("mirror", "slab", "cols"),
            P("mirror", None, None),
            P("mirror", None, None),
            P("mirror", None),
            P(("cols", "slab")),
        ),
        out_specs=P("mirror", "slab", "cols"),
        check_vma=False,
    )
```

```python
import functools

import jax
import jax.numpy as jnp
from jax import lax
from jax.experimental import pallas as pl
from jax.experimental.pallas import tpu as pltpu
from jax.sharding import PartitionSpec as P

MESH = pl.DeviceIdType.MESH
PAIRS = 2
TILE = 256
SWAP_A, SPREAD_A, SPREAD_B, SWAP_B, BACK_SWAP_B, BACK_SPREAD_B, BACK_SPREAD_A, BACK_SWAP_A = range(8)
GROUPS = 8


def split(value):
    high = value.astype(jnp.bfloat16)
    return high, (value - high.astype(jnp.float32)).astype(jnp.bfloat16)


def kernel(
    n,
    field,
    analysis,
    synthesis,
    eigen_in,
    wave_in,
    out,
    own,
    staged,
    matrices,
    swapped_a,
    folded_a,
    landed_a,
    landed_b,
    swapped_b,
    right,
    scaled,
    solved_a,
    solved_b,
    back_a,
    back_swapped_a,
    back_swapped_b,
    combined_b,
    combined_a,
    eigen,
    wave,
    send_sem,
    recv_sem,
    load_sem,
    own_b_sem,
    store_sem,
):
    rows = field.shape[1]
    width = field.shape[2] // n
    w = width // (2 * PAIRS)
    height = analysis.shape[1]
    me = lax.axis_index("slab")
    parity = lax.axis_index("mirror")
    sign = (1 - 2 * parity).astype(jnp.float32)
    partner = {"mirror": 1 - parity}

    digits = [2**b for b in range(n.bit_length() - 1)]
    flips = [digit * (1 - 2 * lax.rem(lax.div(me, digit), 2)) for digit in digits]

    def target(i):
        j, odd = lax.div(i, 2), lax.rem(i, 2)
        mask = (1 - odd) * (n // 2 + j) + odd * (j + 1)
        return me + sum(lax.rem(lax.div(mask, digit), 2) * flip for digit, flip in zip(digits, flips))

    def columns(d, k, b):
        return pl.ds(pl.multiple_of(d * width + (2 * k + b) * w, w), w)

    def remote(src, dst, k, group, received, device):
        return pltpu.make_async_remote_copy(
            src_ref=src,
            dst_ref=dst,
            send_sem=send_sem.at[k * GROUPS + group],
            recv_sem=recv_sem.at[k * GROUPS + group, received],
            device_id=device,
            device_id_type=MESH,
        )

    def swap(src, dst, k, group, d):
        remote(src, dst, k, group, d, partner).start()

    def spread(src, dst, k, group, d):
        remote(src, dst, k, group, me, {"slab": d}).start()

    def arrived(dst, k, group, s):
        remote(dst, dst, k, group, s, partner).wait_recv()

    def each(body, start=0, stop=n - 1):
        def step(i, carry):
            body(i)
            return carry

        lax.fori_loop(start, stop, step, 0)

    def whole(relay):
        body, last = relay
        each(body)
        last()

    loads = [
        pltpu.make_async_copy(field.at[0], own, load_sem.at[0]),
        pltpu.make_async_copy(analysis.at[0], staged.at[0], load_sem.at[1]),
        pltpu.make_async_copy(synthesis.at[0], staged.at[1], load_sem.at[2]),
        pltpu.make_async_copy(eigen_in, eigen, load_sem.at[3]),
        pltpu.make_async_copy(wave_in, wave, load_sem.at[4]),
    ]
    own_b = [
        pltpu.make_async_copy(field.at[0, :, columns(me, k, 1)], landed_b.at[k, me], own_b_sem.at[k])
        for k in range(PAIRS)
    ]
    barrier = pltpu.get_barrier_semaphore()

    def greet(i):
        pl.semaphore_signal(barrier, inc=1, device_id={"slab": target(i)}, device_id_type=MESH)

    each(greet)
    pl.semaphore_signal(barrier, inc=1, device_id=partner, device_id_type=MESH)
    pl.semaphore_wait(barrier, n)

    def forward_start(k):
        def body(i):
            d = target(i)
            swap(field.at[0, :, columns(d, k, 0)], swapped_a.at[k, d], k, SWAP_A, d)
            spread(field.at[0, :, columns(d, k, 1)], landed_b.at[k, me], k, SPREAD_B, d)

        each(body)
        swap(field.at[0, :, columns(me, k, 0)], swapped_a.at[k, me], k, SWAP_A, me)
        swap(field.at[0, :, columns(me, k, 1)], swapped_b.at[k, me], k, SWAP_B, me)

    def fold_a(k, d):
        arrived(swapped_a.at[k, d], k, SWAP_A, d)
        return (swapped_a[k, d] + sign * own[:, columns(d, k, 0)]) * 0.5

    def forward_relay(k):
        def body(i):
            d = target(i)
            folded_a[k, d] = fold_a(k, d)
            spread(folded_a.at[k, d], landed_a.at[k, me], k, SPREAD_A, d)
            s = d
            arrived(landed_b.at[k, s], k, SPREAD_B, s)
            swap(landed_b.at[k, s], swapped_b.at[k, s], k, SWAP_B, s)

        def last():
            landed_a[k, me] = fold_a(k, me)
            own_b[k].wait()

        return body, last

    def gather(k):
        def put(s):
            block = pl.ds(pl.multiple_of(s * rows, rows), rows)
            right[0, block, :w], right[1, block, :w] = split(landed_a[k, s])
            arrived(swapped_b.at[k, s], k, SWAP_B, s)
            folded = (swapped_b[k, s] + sign * landed_b[k, s]) * 0.5
            right[0, block, w:], right[1, block, w:] = split(folded)

        put(me)

        def body(i):
            s = target(i)
            arrived(landed_a.at[k, s], k, SPREAD_A, s)
            put(s)

        each(body)

    tiles = height // TILE

    def product(which, operand, finish, beside):
        def step(t, carry):
            block = pl.ds(pl.multiple_of(t * TILE, TILE), TILE)
            high, low = matrices[which, 0, block, :], matrices[which, 1, block, :]
            dot = functools.partial(jnp.dot, preferred_element_type=jnp.float32)
            finish(t, block, dot(high, operand[0]) + (dot(high, operand[1]) + dot(low, operand[0])))
            at = which * tiles + t
            each(beside, at * (n - 1) // (2 * tiles), (at + 1) * (n - 1) // (2 * tiles))
            return carry

        lax.fori_loop(0, tiles, step, 0)

    def compute(k, relay):
        beside, last = relay

        def scale(t, block, total):
            shift = jnp.broadcast_to(eigen[0:1, block], (2 * w, TILE)).T
            value = total / (shift + wave[0:1, 2 * w * k : 2 * w * (k + 1)])
            scaled[0, block, :], scaled[1, block, :] = split(value)

        def keep(t, block, total):
            per = TILE // rows
            blocks = pl.ds(t * per, per)
            solved_a[k, blocks] = -total[:, :w].reshape(per, rows, w)
            solved_b[k, blocks] = -total[:, w:].reshape(per, rows, w)

        product(0, right, scale, beside)
        product(1, scaled, keep, beside)
        last()

    def back_start(k):
        def body(i):
            d = target(i)
            spread(solved_a.at[k, d], back_a.at[k, me], k, BACK_SPREAD_A, d)
            swap(solved_b.at[k, d], back_swapped_b.at[k, d], k, BACK_SWAP_B, d)

        each(body)
        swap(solved_a.at[k, me], back_swapped_a.at[k, me], k, BACK_SWAP_A, me)
        swap(solved_b.at[k, me], back_swapped_b.at[k, me], k, BACK_SWAP_B, me)

    def combine_b(k, d):
        arrived(back_swapped_b.at[k, d], k, BACK_SWAP_B, d)
        combined_b[k, d] = back_swapped_b[k, d] + sign * solved_b[k, d]

    def own_back_b(k):
        return pltpu.make_async_copy(
            combined_b.at[k, me], out.at[0, :, columns(me, k, 1)], store_sem.at[k, n]
        )

    def back_relay(k):
        def body(i):
            d = target(i)
            combine_b(k, d)
            spread(combined_b.at[k, d], out.at[0, :, columns(me, k, 1)], k, BACK_SPREAD_B, d)
            s = d
            arrived(back_a.at[k, s], k, BACK_SPREAD_A, s)
            swap(back_a.at[k, s], back_swapped_a.at[k, s], k, BACK_SWAP_A, s)

        def last():
            combine_b(k, me)
            own_back_b(k).start()

        return body, last

    def store_a(k, s):
        return pltpu.make_async_copy(
            combined_a.at[k, s], out.at[0, :, columns(s, k, 0)], store_sem.at[k, s]
        )

    def finish(k):
        def put(s, mine):
            arrived(back_swapped_a.at[k, s], k, BACK_SWAP_A, s)
            combined_a[k, s] = back_swapped_a[k, s] + sign * mine[k, s]
            store_a(k, s).start()

        put(me, solved_a)
        each(lambda i: put(target(i), back_a))

    def sent(k, *groups):
        for group in groups:
            swaps = group in (SWAP_A, SWAP_B, BACK_SWAP_A, BACK_SWAP_B)
            pieces = landed_a.at[k, pl.ds(0, n if swaps else n - 1)]
            remote(pieces, pieces, k, group, 0, partner).wait_send()

    def drain(k):
        def body(i):
            s = target(i)
            arrived(out.at[0, :, columns(s, k, 1)], k, BACK_SPREAD_B, s)
            store_a(k, s).wait()

        each(body)
        store_a(k, me).wait()
        own_back_b(k).wait()

    forward_start(0)
    for copy in loads + own_b:
        copy.start()

    def halve(t, carry):
        block = pl.ds(pl.multiple_of(t * TILE, TILE), TILE)
        for which in range(2):
            matrices[which, 0, block, :], matrices[which, 1, block, :] = split(staged[which, block, :])
        return carry

    loads[0].wait()
    whole(forward_relay(0))
    forward_start(1)
    for copy in loads[1:]:
        copy.wait()
    lax.fori_loop(0, tiles, halve, 0)
    gather(0)
    compute(0, forward_relay(1))
    back_start(0)
    gather(1)
    compute(1, back_relay(0))
    back_start(1)
    for k in range(PAIRS):
        sent(k, SWAP_A, SPREAD_A, SPREAD_B, SWAP_B)
    whole(back_relay(1))
    finish(0)
    sent(0, BACK_SWAP_B, BACK_SPREAD_B, BACK_SPREAD_A, BACK_SWAP_A)
    drain(0)
    sent(1, BACK_SWAP_B, BACK_SPREAD_A)
    finish(1)
    drain(1)
    sent(1, BACK_SPREAD_B, BACK_SWAP_A)


def shards(n, right_side, analysis, synthesis, negated_eigen, wave_square):
    rows, modes = right_side.shape[1:]
    height = analysis.shape[1]
    width = modes // n
    w = width // (2 * PAIRS)
    scratch_bytes = 4 * (modes * rows * 7 + height * height * 4 + height * w * 4)
    pieces = pltpu.VMEM((PAIRS, n, rows, w), jnp.float32)
    anywhere = pl.BlockSpec(memory_space=pl.ANY)
    hbm = pl.BlockSpec(memory_space=pltpu.HBM)
    return pl.pallas_call(
        functools.partial(kernel, n),
        out_shape=jax.ShapeDtypeStruct(right_side.shape, jnp.float32),
        in_specs=[hbm] * 5,
        out_specs=anywhere,
        scratch_shapes=[
            pltpu.VMEM((rows, modes), jnp.float32),
            pltpu.VMEM((2, height, height), jnp.float32),
            pltpu.VMEM((2, 2, height, height), jnp.bfloat16),
        ]
        + [pieces] * 5
        + [pltpu.VMEM((2, height, 2 * w), jnp.bfloat16)] * 2
        + [pieces] * 7
        + [
            pltpu.VMEM((1, height), jnp.float32),
            pltpu.VMEM((1, width), jnp.float32),
            pltpu.SemaphoreType.DMA((PAIRS * GROUPS,)),
            pltpu.SemaphoreType.DMA((PAIRS * GROUPS, n)),
            pltpu.SemaphoreType.DMA((5,)),
            pltpu.SemaphoreType.DMA((PAIRS,)),
            pltpu.SemaphoreType.DMA((PAIRS, n + 1)),
        ],
        compiler_params=pltpu.CompilerParams(
            collective_id=0, has_side_effects=True, vmem_limit_bytes=scratch_bytes + 4 * 2**20
        ),
    )(*(
        pltpu.with_memory_space_constraint(value, pltpu.HBM)
        for value in (right_side, analysis, synthesis, negated_eigen, wave_square[None])
    ))


def solution(mesh):
    return jax.shard_map(
        functools.partial(shards, mesh.shape["slab"]),
        mesh=mesh,
        in_specs=(
            P("mirror", "slab", "cols"),
            P("mirror", None, None),
            P("mirror", None, None),
            P("mirror", None),
            P(("cols", "slab")),
        ),
        out_specs=P("mirror", "slab", "cols"),
        check_vma=False,
    )
```

```python
import functools

import jax
import jax.numpy as jnp
from jax import lax
from jax.experimental import pallas as pl
from jax.experimental.pallas import tpu as pltpu
from jax.sharding import PartitionSpec as P

MESH = pl.DeviceIdType.MESH
PAIRS = 2
TILE = 256
STRIPS = 4
SWAP_A, SPREAD_A, SPREAD_B, SWAP_B, BACK_SWAP_B, BACK_SPREAD_B, BACK_SPREAD_A, BACK_SWAP_A = range(8)
GROUPS = 8


def split(value):
    high = value.astype(jnp.bfloat16)
    return high, (value - high.astype(jnp.float32)).astype(jnp.bfloat16)


def kernel(
    n,
    field,
    analysis,
    synthesis,
    eigen_in,
    wave_in,
    out,
    own,
    staged,
    matrices,
    swapped_a,
    folded_a,
    landed_a,
    landed_b,
    swapped_b,
    right,
    scaled,
    solved_a,
    solved_b,
    back_a,
    back_swapped_a,
    back_swapped_b,
    combined_b,
    combined_a,
    eigen,
    wave,
    send_sem,
    recv_sem,
    load_sem,
    own_b_sem,
    store_sem,
):
    rows = field.shape[1]
    width = field.shape[2] // n
    w = width // (2 * PAIRS)
    height = analysis.shape[1]
    me = lax.axis_index("slab")
    parity = lax.axis_index("mirror")
    sign = (1 - 2 * parity).astype(jnp.float32)
    partner = {"mirror": 1 - parity}

    def offset(i):
        half = (i + 1) // 2
        odd = i % 2
        return n // 2 + odd * half + (1 - odd) * (n - half)

    def target(i):
        return lax.rem(me + offset(i), n)

    def source(i):
        return lax.rem(me + 2 * n - offset(i), n)

    def columns(d, k, b):
        return pl.ds(pl.multiple_of(d * width + (2 * k + b) * w, w), w)

    def remote(src, dst, k, group, received, device):
        return pltpu.make_async_remote_copy(
            src_ref=src,
            dst_ref=dst,
            send_sem=send_sem.at[k * GROUPS + group],
            recv_sem=recv_sem.at[k * GROUPS + group, received],
            device_id=device,
            device_id_type=MESH,
        )

    def swap(src, dst, k, group, d):
        remote(src, dst, k, group, d, partner).start()

    def spread(src, dst, k, group, d):
        remote(src, dst, k, group, me, {"slab": d}).start()

    def arrived(dst, k, group, s):
        remote(dst, dst, k, group, s, partner).wait_recv()

    def each(body, start=0, stop=n - 1):
        def step(i, carry):
            body(i)
            return carry

        lax.fori_loop(start, stop, step, 0)

    def whole(relay):
        body, last = relay
        each(body)
        last()

    loads = [
        pltpu.make_async_copy(field.at[0], own, load_sem.at[0]),
        pltpu.make_async_copy(analysis.at[0], staged.at[0], load_sem.at[1]),
        pltpu.make_async_copy(synthesis.at[0], staged.at[1], load_sem.at[2]),
        pltpu.make_async_copy(eigen_in, eigen, load_sem.at[3]),
        pltpu.make_async_copy(wave_in, wave, load_sem.at[4]),
    ]
    own_b = [
        pltpu.make_async_copy(field.at[0, :, columns(me, k, 1)], landed_b.at[k, me], own_b_sem.at[k])
        for k in range(PAIRS)
    ]
    barrier = pltpu.get_barrier_semaphore()

    def greet(i):
        pl.semaphore_signal(barrier, inc=1, device_id={"slab": target(i)}, device_id_type=MESH)

    pl.semaphore_signal(barrier, inc=1, device_id=partner, device_id_type=MESH)
    each(greet)
    pl.semaphore_wait(barrier, n)

    def forward_start(k):
        def body(i):
            d = target(i)
            swap(field.at[0, :, columns(d, k, 0)], swapped_a.at[k, d], k, SWAP_A, d)
            spread(field.at[0, :, columns(d, k, 1)], landed_b.at[k, me], k, SPREAD_B, d)

        each(body)
        swap(field.at[0, :, columns(me, k, 0)], swapped_a.at[k, me], k, SWAP_A, me)
        swap(field.at[0, :, columns(me, k, 1)], swapped_b.at[k, me], k, SWAP_B, me)

    def fold_a(k, d):
        arrived(swapped_a.at[k, d], k, SWAP_A, d)
        return (swapped_a[k, d] + sign * own[:, columns(d, k, 0)]) * 0.5

    def forward_relay(k):
        def body(i):
            d = target(i)
            folded_a[k, d] = fold_a(k, d)
            spread(folded_a.at[k, d], landed_a.at[k, me], k, SPREAD_A, d)
            s = source(i)
            arrived(landed_b.at[k, s], k, SPREAD_B, s)
            swap(landed_b.at[k, s], swapped_b.at[k, s], k, SWAP_B, s)

        def last():
            landed_a[k, me] = fold_a(k, me)
            own_b[k].wait()

        return body, last

    def gather(k):
        def put(s):
            block = pl.ds(pl.multiple_of(s * rows, rows), rows)
            right[0, block, :w], right[1, block, :w] = split(landed_a[k, s])
            arrived(swapped_b.at[k, s], k, SWAP_B, s)
            folded = (swapped_b[k, s] + sign * landed_b[k, s]) * 0.5
            right[0, block, w:], right[1, block, w:] = split(folded)

        put(me)

        def body(i):
            s = source(i)
            arrived(landed_a.at[k, s], k, SPREAD_A, s)
            put(s)

        each(body)

    tiles = height // TILE

    def product(which, operand, finish, beside):
        def step(t, carry):
            block = pl.ds(pl.multiple_of(t * TILE, TILE), TILE)
            high, low = matrices[which, 0, block, :], matrices[which, 1, block, :]
            dot = functools.partial(jnp.dot, preferred_element_type=jnp.float32)
            finish(t, block, dot(high, operand[0]) + (dot(high, operand[1]) + dot(low, operand[0])))
            at = which * tiles + t
            each(beside, at * (n - 1) // (2 * tiles), (at + 1) * (n - 1) // (2 * tiles))
            return carry

        lax.fori_loop(0, tiles, step, 0)

    def compute(k, relay):
        beside, last = relay

        def scale(t, block, total):
            shift = jnp.broadcast_to(eigen[0:1, block], (2 * w, TILE)).T
            value = total / (shift + wave[0:1, 2 * w * k : 2 * w * (k + 1)])
            scaled[0, block, :], scaled[1, block, :] = split(value)

        def keep(t, block, total):
            per = TILE // rows
            blocks = pl.ds(t * per, per)
            solved_a[k, blocks] = -total[:, :w].reshape(per, rows, w)
            solved_b[k, blocks] = -total[:, w:].reshape(per, rows, w)

        product(0, right, scale, beside)
        product(1, scaled, keep, beside)
        last()

    def back_start(k):
        def body(i):
            d = target(i)
            spread(solved_a.at[k, d], back_a.at[k, me], k, BACK_SPREAD_A, d)
            swap(solved_b.at[k, d], back_swapped_b.at[k, d], k, BACK_SWAP_B, d)

        each(body)
        swap(solved_a.at[k, me], back_swapped_a.at[k, me], k, BACK_SWAP_A, me)
        swap(solved_b.at[k, me], back_swapped_b.at[k, me], k, BACK_SWAP_B, me)

    def combine_b(k, d):
        arrived(back_swapped_b.at[k, d], k, BACK_SWAP_B, d)
        combined_b[k, d] = back_swapped_b[k, d] + sign * solved_b[k, d]

    def own_back_b(k):
        return pltpu.make_async_copy(
            combined_b.at[k, me], out.at[0, :, columns(me, k, 1)], store_sem.at[k, 1]
        )

    def back_relay(k):
        def body(i):
            d = target(i)
            combine_b(k, d)
            remote(
                combined_b.at[k, d], out.at[0, :, columns(me, k, 1)], k, BACK_SPREAD_B, 0, {"slab": d}
            ).start()
            s = source(i)
            arrived(back_a.at[k, s], k, BACK_SPREAD_A, s)
            swap(back_a.at[k, s], back_swapped_a.at[k, s], k, BACK_SWAP_A, s)

        def last():
            combine_b(k, me)
            own_back_b(k).start()

        return body, last

    def store_a(k, s):
        return pltpu.make_async_copy(
            combined_a.at[k, s], out.at[0, :, columns(s, k, 0)], store_sem.at[k, 0]
        )

    def finish(k):
        def put(s, mine):
            arrived(back_swapped_a.at[k, s], k, BACK_SWAP_A, s)
            combined_a[k, s] = back_swapped_a[k, s] + sign * mine[k, s]
            store_a(k, s).start()

        put(me, solved_a)
        each(lambda i: put(source(i), back_a))

    def sent(k, *groups):
        for group in groups:
            swaps = group in (SWAP_A, SWAP_B, BACK_SWAP_A, BACK_SWAP_B)
            pieces = landed_a.at[k, pl.ds(0, n if swaps else n - 1)]
            remote(pieces, pieces, k, group, 0, partner).wait_send()

    def drain(k):
        pieces = landed_a.at[k, pl.ds(0, n - 1)]
        remote(pieces, pieces, k, BACK_SPREAD_B, 0, partner).wait_recv()
        own_back_b(k).wait()
        pltpu.make_async_copy(combined_a.at[k], combined_a.at[k], store_sem.at[k, 0]).wait()

    forward_start(0)
    for copy in loads + own_b:
        copy.start()

    def halve(t, carry):
        block = pl.ds(pl.multiple_of(t * TILE, TILE), TILE)
        for which in range(2):
            matrices[which, 0, block, :], matrices[which, 1, block, :] = split(staged[which, block, :])
        return carry

    loads[0].wait()
    whole(forward_relay(0))
    forward_start(1)
    for copy in loads[1:]:
        copy.wait()
    lax.fori_loop(0, tiles, halve, 0)
    gather(0)
    compute(0, forward_relay(1))
    back_start(0)
    gather(1)
    compute(1, back_relay(0))
    back_start(1)
    for k in range(PAIRS):
        sent(k, SWAP_A, SPREAD_A, SPREAD_B, SWAP_B)
    whole(back_relay(1))
    finish(0)
    sent(0, BACK_SWAP_B, BACK_SPREAD_B, BACK_SPREAD_A, BACK_SWAP_A)
    drain(0)
    sent(1, BACK_SWAP_B, BACK_SPREAD_A)
    finish(1)
    drain(1)
    sent(1, BACK_SPREAD_B, BACK_SWAP_A)


def export(held, out, sem):
    rows = held.shape[1] // STRIPS
    copies = [
        pltpu.make_async_copy(
            held.at[0, pl.ds(i * rows, rows)], out.at[0, pl.ds(i * rows, rows)], sem.at[i]
        )
        for i in range(STRIPS)
    ]
    for copy in copies:
        copy.start()
    for copy in copies:
        copy.wait()


def shards(n, right_side, analysis, synthesis, negated_eigen, wave_square):
    rows, modes = right_side.shape[1:]
    height = analysis.shape[1]
    width = modes // n
    w = width // (2 * PAIRS)
    scratch_bytes = 4 * (modes * rows * 7 + height * height * 4 + height * w * 4)
    pieces = pltpu.VMEM((PAIRS, n, rows, w), jnp.float32)
    anywhere = pl.BlockSpec(memory_space=pl.ANY)
    hbm = pl.BlockSpec(memory_space=pltpu.HBM)
    result = pl.pallas_call(
        functools.partial(kernel, n),
        out_shape=jax.ShapeDtypeStruct(right_side.shape, jnp.float32),
        in_specs=[hbm] * 5,
        out_specs=anywhere,
        scratch_shapes=[
            pltpu.VMEM((rows, modes), jnp.float32),
            pltpu.VMEM((2, height, height), jnp.float32),
            pltpu.VMEM((2, 2, height, height), jnp.bfloat16),
        ]
        + [pieces] * 5
        + [pltpu.VMEM((2, height, 2 * w), jnp.bfloat16)] * 2
        + [pieces] * 7
        + [
            pltpu.VMEM((1, height), jnp.float32),
            pltpu.VMEM((1, width), jnp.float32),
            pltpu.SemaphoreType.DMA((PAIRS * GROUPS,)),
            pltpu.SemaphoreType.DMA((PAIRS * GROUPS, n)),
            pltpu.SemaphoreType.DMA((5,)),
            pltpu.SemaphoreType.DMA((PAIRS,)),
            pltpu.SemaphoreType.DMA((PAIRS, 2)),
        ],
        compiler_params=pltpu.CompilerParams(
            collective_id=0, has_side_effects=True, vmem_limit_bytes=scratch_bytes + 4 * 2**20
        ),
    )(*(
        pltpu.with_memory_space_constraint(value, pltpu.HBM)
        for value in (right_side, analysis, synthesis, negated_eigen, wave_square[None])
    ))
    return pl.pallas_call(
        export,
        out_shape=jax.ShapeDtypeStruct(right_side.shape, jnp.float32),
        in_specs=[anywhere],
        out_specs=anywhere,
        scratch_shapes=[pltpu.SemaphoreType.DMA((STRIPS,))],
    )(result)


def solution(mesh):
    return jax.shard_map(
        functools.partial(shards, mesh.shape["slab"]),
        mesh=mesh,
        in_specs=(
            P("mirror", "slab", "cols"),
            P("mirror", None, None),
            P("mirror", None, None),
            P("mirror", None),
            P(("cols", "slab")),
        ),
        out_specs=P("mirror", "slab", "cols"),
        check_vma=False,
    )
```

```python
import functools

import jax
import jax.numpy as jnp
from jax import lax
from jax.experimental import pallas as pl
from jax.experimental.pallas import tpu as pltpu
from jax.sharding import PartitionSpec as P

MESH = pl.DeviceIdType.MESH
PAIRS = 2
TILE = 256
SWAP_A, SPREAD_A, SPREAD_B, SWAP_B, BACK_SWAP_B, BACK_SPREAD_B, BACK_SPREAD_A, BACK_SWAP_A = range(8)
GROUPS = 8


def split(value):
    high = value.astype(jnp.bfloat16)
    return high, (value - high.astype(jnp.float32)).astype(jnp.bfloat16)


def kernel(
    n,
    field,
    analysis,
    synthesis,
    eigen_in,
    wave_in,
    out,
    own,
    staged,
    matrices,
    swapped_a,
    folded_a,
    landed_a,
    landed_b,
    swapped_b,
    right,
    scaled,
    solved_a,
    solved_b,
    back_a,
    back_swapped_a,
    back_swapped_b,
    combined_b,
    combined_a,
    eigen,
    wave,
    send_sem,
    recv_sem,
    load_sem,
    own_b_sem,
    store_sem,
):
    rows = field.shape[1]
    width = field.shape[2] // n
    w = width // (2 * PAIRS)
    height = analysis.shape[1]
    me = lax.axis_index("slab")
    parity = lax.axis_index("mirror")
    sign = (1 - 2 * parity).astype(jnp.float32)
    partner = {"mirror": 1 - parity}

    def offset(i):
        half = (i + 1) // 2
        odd = i % 2
        return n // 2 + odd * half + (1 - odd) * (n - half)

    def target(i):
        return lax.rem(me + offset(i), n)

    def source(i):
        return lax.rem(me + 2 * n - offset(i), n)

    def columns(d, k, b):
        return pl.ds(pl.multiple_of(d * width + (2 * k + b) * w, w), w)

    def remote(src, dst, k, group, received, device):
        return pltpu.make_async_remote_copy(
            src_ref=src,
            dst_ref=dst,
            send_sem=send_sem.at[k * GROUPS + group],
            recv_sem=recv_sem.at[k * GROUPS + group, received],
            device_id=device,
            device_id_type=MESH,
        )

    def swap(src, dst, k, group, d):
        remote(src, dst, k, group, d, partner).start()

    def spread(src, dst, k, group, d):
        remote(src, dst, k, group, me, {"slab": d}).start()

    def arrived(dst, k, group, s):
        remote(dst, dst, k, group, s, partner).wait_recv()

    def each(body, start=0, stop=n - 1):
        def step(i, carry):
            body(i)
            return carry

        lax.fori_loop(start, stop, step, 0)

    def whole(relay):
        body, last = relay
        each(body)
        last()

    loads = [
        pltpu.make_async_copy(field.at[0], own, load_sem.at[0]),
        pltpu.make_async_copy(analysis.at[0], staged.at[0], load_sem.at[1]),
        pltpu.make_async_copy(synthesis.at[0], staged.at[1], load_sem.at[2]),
        pltpu.make_async_copy(eigen_in, eigen, load_sem.at[3]),
        pltpu.make_async_copy(wave_in, wave, load_sem.at[4]),
    ]
    own_b = [
        pltpu.make_async_copy(field.at[0, :, columns(me, k, 1)], landed_b.at[k, me], own_b_sem.at[k])
        for k in range(PAIRS)
    ]
    barrier = pltpu.get_barrier_semaphore()

    def greet(i):
        pl.semaphore_signal(barrier, inc=1, device_id={"slab": target(i)}, device_id_type=MESH)

    pl.semaphore_signal(barrier, inc=1, device_id=partner, device_id_type=MESH)
    each(greet)
    pl.semaphore_wait(barrier, n)

    def forward_start(k):
        def body(i):
            d = target(i)
            swap(field.at[0, :, columns(d, k, 0)], swapped_a.at[k, d], k, SWAP_A, d)
            spread(field.at[0, :, columns(d, k, 1)], landed_b.at[k, me], k, SPREAD_B, d)

        each(body)
        swap(field.at[0, :, columns(me, k, 0)], swapped_a.at[k, me], k, SWAP_A, me)
        swap(field.at[0, :, columns(me, k, 1)], swapped_b.at[k, me], k, SWAP_B, me)

    def fold_a(k, d):
        arrived(swapped_a.at[k, d], k, SWAP_A, d)
        return (swapped_a[k, d] + sign * own[:, columns(d, k, 0)]) * 0.5

    def forward_relay(k):
        def body(i):
            d = target(i)
            folded_a[k, d] = fold_a(k, d)
            spread(folded_a.at[k, d], landed_a.at[k, me], k, SPREAD_A, d)
            s = source(i)
            arrived(landed_b.at[k, s], k, SPREAD_B, s)
            swap(landed_b.at[k, s], swapped_b.at[k, s], k, SWAP_B, s)

        def last():
            landed_a[k, me] = fold_a(k, me)
            own_b[k].wait()

        return body, last

    def gather(k):
        def put(s):
            block = pl.ds(pl.multiple_of(s * rows, rows), rows)
            right[0, block, :w], right[1, block, :w] = split(landed_a[k, s])
            arrived(swapped_b.at[k, s], k, SWAP_B, s)
            folded = (swapped_b[k, s] + sign * landed_b[k, s]) * 0.5
            right[0, block, w:], right[1, block, w:] = split(folded)

        put(me)

        def body(i):
            s = source(i)
            arrived(landed_a.at[k, s], k, SPREAD_A, s)
            put(s)

        each(body)

    tiles = height // TILE

    def product(which, operand, finish, beside):
        def step(t, carry):
            block = pl.ds(pl.multiple_of(t * TILE, TILE), TILE)
            high, low = matrices[which, 0, block, :], matrices[which, 1, block, :]
            dot = functools.partial(jnp.dot, preferred_element_type=jnp.float32)
            finish(t, block, dot(high, operand[0]) + (dot(high, operand[1]) + dot(low, operand[0])))
            at = which * tiles + t
            each(beside, at * (n - 1) // (2 * tiles), (at + 1) * (n - 1) // (2 * tiles))
            return carry

        lax.fori_loop(0, tiles, step, 0)

    def compute(k, relay):
        beside, last = relay

        def scale(t, block, total):
            shift = jnp.broadcast_to(eigen[0:1, block], (2 * w, TILE)).T
            value = total / (shift + wave[0:1, 2 * w * k : 2 * w * (k + 1)])
            scaled[0, block, :], scaled[1, block, :] = split(value)

        def keep(t, block, total):
            per = TILE // rows
            blocks = pl.ds(t * per, per)
            solved_a[k, blocks] = -total[:, :w].reshape(per, rows, w)
            solved_b[k, blocks] = -total[:, w:].reshape(per, rows, w)

        product(0, right, scale, beside)
        product(1, scaled, keep, beside)
        last()

    def back_start(k):
        def body(i):
            d = target(i)
            spread(solved_a.at[k, d], back_a.at[k, me], k, BACK_SPREAD_A, d)
            swap(solved_b.at[k, d], back_swapped_b.at[k, d], k, BACK_SWAP_B, d)

        each(body)
        swap(solved_a.at[k, me], back_swapped_a.at[k, me], k, BACK_SWAP_A, me)
        swap(solved_b.at[k, me], back_swapped_b.at[k, me], k, BACK_SWAP_B, me)

    def combine_b(k, d):
        arrived(back_swapped_b.at[k, d], k, BACK_SWAP_B, d)
        combined_b[k, d] = back_swapped_b[k, d] + sign * solved_b[k, d]

    def own_back_b(k):
        return pltpu.make_async_copy(
            combined_b.at[k, me], out.at[0, :, columns(me, k, 1)], store_sem.at[k, 1]
        )

    def back_relay(k):
        def body(i):
            d = target(i)
            combine_b(k, d)
            remote(
                combined_b.at[k, d], out.at[0, :, columns(me, k, 1)], k, BACK_SPREAD_B, 0, {"slab": d}
            ).start()
            s = source(i)
            arrived(back_a.at[k, s], k, BACK_SPREAD_A, s)
            swap(back_a.at[k, s], back_swapped_a.at[k, s], k, BACK_SWAP_A, s)

        def last():
            combine_b(k, me)
            own_back_b(k).start()

        return body, last

    def store_a(k, s):
        return pltpu.make_async_copy(
            combined_a.at[k, s], out.at[0, :, columns(s, k, 0)], store_sem.at[k, 0]
        )

    def finish(k):
        def put(s, mine):
            arrived(back_swapped_a.at[k, s], k, BACK_SWAP_A, s)
            combined_a[k, s] = back_swapped_a[k, s] + sign * mine[k, s]
            store_a(k, s).start()

        put(me, solved_a)
        each(lambda i: put(source(i), back_a))

    def sent(k, *groups):
        for group in groups:
            swaps = group in (SWAP_A, SWAP_B, BACK_SWAP_A, BACK_SWAP_B)
            pieces = landed_a.at[k, pl.ds(0, n if swaps else n - 1)]
            remote(pieces, pieces, k, group, 0, partner).wait_send()

    def drain(k):
        pieces = landed_a.at[k, pl.ds(0, n - 1)]
        remote(pieces, pieces, k, BACK_SPREAD_B, 0, partner).wait_recv()
        own_back_b(k).wait()
        pltpu.make_async_copy(combined_a.at[k], combined_a.at[k], store_sem.at[k, 0]).wait()

    forward_start(0)
    for copy in loads + own_b:
        copy.start()

    def halve(t, carry):
        block = pl.ds(pl.multiple_of(t * TILE, TILE), TILE)
        for which in range(2):
            matrices[which, 0, block, :], matrices[which, 1, block, :] = split(staged[which, block, :])
        return carry

    loads[0].wait()
    whole(forward_relay(0))
    forward_start(1)
    for copy in loads[1:]:
        copy.wait()
    lax.fori_loop(0, tiles, halve, 0)
    gather(0)
    compute(0, forward_relay(1))
    back_start(0)
    gather(1)
    compute(1, back_relay(0))
    back_start(1)
    for k in range(PAIRS):
        sent(k, SWAP_A, SPREAD_A, SPREAD_B, SWAP_B)
    whole(back_relay(1))
    finish(0)
    sent(0, BACK_SWAP_B, BACK_SPREAD_B, BACK_SPREAD_A, BACK_SWAP_A)
    drain(0)
    sent(1, BACK_SWAP_B, BACK_SPREAD_A)
    finish(1)
    drain(1)
    sent(1, BACK_SPREAD_B, BACK_SWAP_A)


def shards(n, right_side, analysis, synthesis, negated_eigen, wave_square):
    rows, modes = right_side.shape[1:]
    height = analysis.shape[1]
    width = modes // n
    w = width // (2 * PAIRS)
    scratch_bytes = 4 * (modes * rows * 7 + height * height * 4 + height * w * 4)
    pieces = pltpu.VMEM((PAIRS, n, rows, w), jnp.float32)
    anywhere = pl.BlockSpec(memory_space=pl.ANY)
    hbm = pl.BlockSpec(memory_space=pltpu.HBM)
    return pl.pallas_call(
        functools.partial(kernel, n),
        out_shape=jax.ShapeDtypeStruct(right_side.shape, jnp.float32),
        in_specs=[hbm] * 5,
        out_specs=anywhere,
        scratch_shapes=[
            pltpu.VMEM((rows, modes), jnp.float32),
            pltpu.VMEM((2, height, height), jnp.float32),
            pltpu.VMEM((2, 2, height, height), jnp.bfloat16),
        ]
        + [pieces] * 5
        + [pltpu.VMEM((2, height, 2 * w), jnp.bfloat16)] * 2
        + [pieces] * 7
        + [
            pltpu.VMEM((1, height), jnp.float32),
            pltpu.VMEM((1, width), jnp.float32),
            pltpu.SemaphoreType.DMA((PAIRS * GROUPS,)),
            pltpu.SemaphoreType.DMA((PAIRS * GROUPS, n)),
            pltpu.SemaphoreType.DMA((5,)),
            pltpu.SemaphoreType.DMA((PAIRS,)),
            pltpu.SemaphoreType.DMA((PAIRS, 2)),
        ],
        compiler_params=pltpu.CompilerParams(
            collective_id=0, has_side_effects=True, vmem_limit_bytes=scratch_bytes + 4 * 2**20
        ),
    )(*(
        pltpu.with_memory_space_constraint(value, pltpu.HBM)
        for value in (right_side, analysis, synthesis, negated_eigen, wave_square[None])
    ))


def solution(mesh):
    return jax.shard_map(
        functools.partial(shards, mesh.shape["slab"]),
        mesh=mesh,
        in_specs=(
            P("mirror", "slab", "cols"),
            P("mirror", None, None),
            P("mirror", None, None),
            P("mirror", None),
            P(("cols", "slab")),
        ),
        out_specs=P("mirror", "slab", "cols"),
        check_vma=False,
    )
```

```python
import functools

import jax
import jax.numpy as jnp
from jax import lax
from jax.experimental import pallas as pl
from jax.experimental.pallas import tpu as pltpu
from jax.sharding import PartitionSpec as P

MESH = pl.DeviceIdType.MESH
PAIRS = 2
TILE = 256
SWAP_A, SPREAD_A, SPREAD_B, SWAP_B, BACK_SWAP_B, BACK_SPREAD_B, BACK_SPREAD_A, BACK_SWAP_A = range(8)
GROUPS = 8


def split(value):
    high = value.astype(jnp.bfloat16)
    return high, (value - high.astype(jnp.float32)).astype(jnp.bfloat16)


def kernel(
    n,
    field,
    analysis,
    synthesis,
    eigen_in,
    wave_in,
    out,
    own,
    staged,
    matrices,
    swapped_a,
    folded_a,
    landed_a,
    landed_b,
    swapped_b,
    right,
    scaled,
    solved_a,
    solved_b,
    back_a,
    back_swapped_a,
    back_swapped_b,
    combined_b,
    combined_a,
    eigen,
    wave,
    send_sem,
    recv_sem,
    load_sem,
    own_b_sem,
    store_sem,
):
    rows = field.shape[1]
    width = field.shape[2] // n
    w = width // (2 * PAIRS)
    height = analysis.shape[1]
    me = lax.axis_index("slab")
    parity = lax.axis_index("mirror")
    sign = (1 - 2 * parity).astype(jnp.float32)
    partner = {"mirror": 1 - parity}

    def offset(i):
        half = (i + 1) // 2
        odd = i % 2
        return n // 2 + odd * half + (1 - odd) * (n - half)

    def target(i):
        return lax.rem(me + offset(i), n)

    def source(i):
        return lax.rem(me + 2 * n - offset(i), n)

    def columns(d, k, b):
        return pl.ds(pl.multiple_of(d * width + (2 * k + b) * w, w), w)

    def remote(src, dst, k, group, received, device):
        return pltpu.make_async_remote_copy(
            src_ref=src,
            dst_ref=dst,
            send_sem=send_sem.at[k * GROUPS + group],
            recv_sem=recv_sem.at[k * GROUPS + group, received],
            device_id=device,
            device_id_type=MESH,
        )

    def swap(src, dst, k, group, d):
        remote(src, dst, k, group, d, partner).start()

    def spread(src, dst, k, group, d):
        remote(src, dst, k, group, me, {"slab": d}).start()

    def arrived(dst, k, group, s):
        remote(dst, dst, k, group, s, partner).wait_recv()

    def each(body, start=0, stop=n - 1):
        def step(i, carry):
            body(i)
            return carry

        lax.fori_loop(start, stop, step, 0)

    def whole(relay):
        body, last = relay
        each(body)
        last()

    loads = [
        pltpu.make_async_copy(field.at[0], own, load_sem.at[0]),
        pltpu.make_async_copy(analysis.at[0], staged.at[0], load_sem.at[1]),
        pltpu.make_async_copy(synthesis.at[0], staged.at[1], load_sem.at[2]),
        pltpu.make_async_copy(eigen_in, eigen, load_sem.at[3]),
        pltpu.make_async_copy(wave_in, wave, load_sem.at[4]),
    ]
    own_b = [
        pltpu.make_async_copy(field.at[0, :, columns(me, k, 1)], landed_b.at[k, me], own_b_sem.at[k])
        for k in range(PAIRS)
    ]
    barrier = pltpu.get_barrier_semaphore()

    def greet(i):
        pl.semaphore_signal(barrier, inc=1, device_id={"slab": target(i)}, device_id_type=MESH)

    pl.semaphore_signal(barrier, inc=1, device_id=partner, device_id_type=MESH)
    each(greet)
    pl.semaphore_wait(barrier, n)

    def forward_start(k):
        def body(i):
            d = target(i)
            swap(field.at[0, :, columns(d, k, 0)], swapped_a.at[k, d], k, SWAP_A, d)
            spread(field.at[0, :, columns(d, k, 1)], landed_b.at[k, me], k, SPREAD_B, d)

        each(body)
        swap(field.at[0, :, columns(me, k, 0)], swapped_a.at[k, me], k, SWAP_A, me)
        swap(field.at[0, :, columns(me, k, 1)], swapped_b.at[k, me], k, SWAP_B, me)

    def fold_a(k, d):
        arrived(swapped_a.at[k, d], k, SWAP_A, d)
        return (swapped_a[k, d] + sign * own[:, columns(d, k, 0)]) * 0.5

    def forward_relay(k):
        def body(i):
            s = source(i)
            arrived(landed_b.at[k, s], k, SPREAD_B, s)
            swap(landed_b.at[k, s], swapped_b.at[k, s], k, SWAP_B, s)
            d = target(i)
            folded_a[k, d] = fold_a(k, d)
            spread(folded_a.at[k, d], landed_a.at[k, me], k, SPREAD_A, d)

        def last():
            landed_a[k, me] = fold_a(k, me)
            own_b[k].wait()

        return body, last

    def gather(k):
        def put(s):
            block = pl.ds(pl.multiple_of(s * rows, rows), rows)
            right[0, block, :w], right[1, block, :w] = split(landed_a[k, s])
            arrived(swapped_b.at[k, s], k, SWAP_B, s)
            folded = (swapped_b[k, s] + sign * landed_b[k, s]) * 0.5
            right[0, block, w:], right[1, block, w:] = split(folded)

        put(me)

        def body(i):
            s = source(i)
            arrived(landed_a.at[k, s], k, SPREAD_A, s)
            put(s)

        each(body)

    tiles = height // TILE

    def product(which, operand, finish, beside):
        def step(t, carry):
            block = pl.ds(pl.multiple_of(t * TILE, TILE), TILE)
            high, low = matrices[which, 0, block, :], matrices[which, 1, block, :]
            dot = functools.partial(jnp.dot, preferred_element_type=jnp.float32)
            finish(t, block, dot(high, operand[0]) + (dot(high, operand[1]) + dot(low, operand[0])))
            at = which * tiles + t
            each(beside, at * (n - 1) // (2 * tiles), (at + 1) * (n - 1) // (2 * tiles))
            return carry

        lax.fori_loop(0, tiles, step, 0)

    def compute(k, relay):
        beside, last = relay

        def scale(t, block, total):
            shift = jnp.broadcast_to(eigen[0:1, block], (2 * w, TILE)).T
            value = total / (shift + wave[0:1, 2 * w * k : 2 * w * (k + 1)])
            scaled[0, block, :], scaled[1, block, :] = split(value)

        def keep(t, block, total):
            per = TILE // rows
            blocks = pl.ds(t * per, per)
            solved_a[k, blocks] = -total[:, :w].reshape(per, rows, w)
            solved_b[k, blocks] = -total[:, w:].reshape(per, rows, w)

        product(0, right, scale, beside)
        product(1, scaled, keep, beside)
        last()

    def back_start(k):
        def body(i):
            d = target(i)
            spread(solved_a.at[k, d], back_a.at[k, me], k, BACK_SPREAD_A, d)
            swap(solved_b.at[k, d], back_swapped_b.at[k, d], k, BACK_SWAP_B, d)

        each(body)
        swap(solved_a.at[k, me], back_swapped_a.at[k, me], k, BACK_SWAP_A, me)
        swap(solved_b.at[k, me], back_swapped_b.at[k, me], k, BACK_SWAP_B, me)

    def combine_b(k, d):
        arrived(back_swapped_b.at[k, d], k, BACK_SWAP_B, d)
        combined_b[k, d] = back_swapped_b[k, d] + sign * solved_b[k, d]

    def own_back_b(k):
        return pltpu.make_async_copy(
            combined_b.at[k, me], out.at[0, :, columns(me, k, 1)], store_sem.at[k, 1]
        )

    def back_relay(k):
        def body(i):
            s = source(i)
            arrived(back_a.at[k, s], k, BACK_SPREAD_A, s)
            swap(back_a.at[k, s], back_swapped_a.at[k, s], k, BACK_SWAP_A, s)
            d = target(i)
            combine_b(k, d)
            remote(
                combined_b.at[k, d], out.at[0, :, columns(me, k, 1)], k, BACK_SPREAD_B, 0, {"slab": d}
            ).start()

        def last():
            combine_b(k, me)
            own_back_b(k).start()

        return body, last

    def store_a(k, s):
        return pltpu.make_async_copy(
            combined_a.at[k, s], out.at[0, :, columns(s, k, 0)], store_sem.at[k, 0]
        )

    def finish(k):
        def put(s, mine):
            arrived(back_swapped_a.at[k, s], k, BACK_SWAP_A, s)
            combined_a[k, s] = back_swapped_a[k, s] + sign * mine[k, s]
            store_a(k, s).start()

        put(me, solved_a)
        each(lambda i: put(source(i), back_a))

    def sent(k, *groups):
        for group in groups:
            swaps = group in (SWAP_A, SWAP_B, BACK_SWAP_A, BACK_SWAP_B)
            pieces = landed_a.at[k, pl.ds(0, n if swaps else n - 1)]
            remote(pieces, pieces, k, group, 0, partner).wait_send()

    def drain(k):
        pieces = landed_a.at[k, pl.ds(0, n - 1)]
        remote(pieces, pieces, k, BACK_SPREAD_B, 0, partner).wait_recv()
        own_back_b(k).wait()
        pltpu.make_async_copy(combined_a.at[k], combined_a.at[k], store_sem.at[k, 0]).wait()

    forward_start(0)
    for copy in loads + own_b:
        copy.start()

    def halve(t, carry):
        block = pl.ds(pl.multiple_of(t * TILE, TILE), TILE)
        for which in range(2):
            matrices[which, 0, block, :], matrices[which, 1, block, :] = split(staged[which, block, :])
        return carry

    loads[0].wait()
    whole(forward_relay(0))
    forward_start(1)
    for copy in loads[1:]:
        copy.wait()
    lax.fori_loop(0, tiles, halve, 0)
    gather(0)
    compute(0, forward_relay(1))
    back_start(0)
    gather(1)
    compute(1, back_relay(0))
    back_start(1)
    for k in range(PAIRS):
        sent(k, SWAP_A, SPREAD_A, SPREAD_B, SWAP_B)
    whole(back_relay(1))
    finish(0)
    sent(0, BACK_SWAP_B, BACK_SPREAD_B, BACK_SPREAD_A, BACK_SWAP_A)
    drain(0)
    sent(1, BACK_SWAP_B, BACK_SPREAD_A)
    finish(1)
    drain(1)
    sent(1, BACK_SPREAD_B, BACK_SWAP_A)


def shards(n, right_side, analysis, synthesis, negated_eigen, wave_square):
    rows, modes = right_side.shape[1:]
    height = analysis.shape[1]
    width = modes // n
    w = width // (2 * PAIRS)
    scratch_bytes = 4 * (modes * rows * 7 + height * height * 4 + height * w * 4)
    pieces = pltpu.VMEM((PAIRS, n, rows, w), jnp.float32)
    anywhere = pl.BlockSpec(memory_space=pl.ANY)
    hbm = pl.BlockSpec(memory_space=pltpu.HBM)
    return pl.pallas_call(
        functools.partial(kernel, n),
        out_shape=jax.ShapeDtypeStruct(right_side.shape, jnp.float32),
        in_specs=[hbm] * 5,
        out_specs=anywhere,
        scratch_shapes=[
            pltpu.VMEM((rows, modes), jnp.float32),
            pltpu.VMEM((2, height, height), jnp.float32),
            pltpu.VMEM((2, 2, height, height), jnp.bfloat16),
        ]
        + [pieces] * 5
        + [pltpu.VMEM((2, height, 2 * w), jnp.bfloat16)] * 2
        + [pieces] * 7
        + [
            pltpu.VMEM((1, height), jnp.float32),
            pltpu.VMEM((1, width), jnp.float32),
            pltpu.SemaphoreType.DMA((PAIRS * GROUPS,)),
            pltpu.SemaphoreType.DMA((PAIRS * GROUPS, n)),
            pltpu.SemaphoreType.DMA((5,)),
            pltpu.SemaphoreType.DMA((PAIRS,)),
            pltpu.SemaphoreType.DMA((PAIRS, 2)),
        ],
        compiler_params=pltpu.CompilerParams(
            collective_id=0, has_side_effects=True, vmem_limit_bytes=scratch_bytes + 4 * 2**20
        ),
    )(*(
        pltpu.with_memory_space_constraint(value, pltpu.HBM)
        for value in (right_side, analysis, synthesis, negated_eigen, wave_square[None])
    ))


def solution(mesh):
    return jax.shard_map(
        functools.partial(shards, mesh.shape["slab"]),
        mesh=mesh,
        in_specs=(
            P("mirror", "slab", "cols"),
            P("mirror", None, None),
            P("mirror", None, None),
            P("mirror", None),
            P(("cols", "slab")),
        ),
        out_specs=P("mirror", "slab", "cols"),
        check_vma=False,
    )
```
